256 devices in a mesh: section: 2 (over y_hi), dp: 16 (over y_lo, x, core), mp: 8 (over z).
Axes of the slice: x: 4, y: 4 (y_hi: 2, y_lo: 2; y = y_hi * 2 + y_lo), z: 8, core: 2. Of those that a mesh axis runs over, the one named last changes fastest.
Arguments:
- activations: bfloat16 [2, 1024, 4096], P(None, 'dp'), may hold values from -6 to 6
- cotangent: bfloat16 [2, 1024, 4096], P(None, 'dp'), may hold values from -6 to 6
- norm_gain: float32 [2, 4096], P('section'), may hold values from 0.1 to 1.9
- w_up: bfloat16 [2, 4096, 8192], P('section', 'dp', 'mp'), may hold values from -0.09375 to 0.09375
- w_down: bfloat16 [2, 4096, 8192], P('section', 'dp', 'mp'), may hold values from -0.0625 to 0.0625
- gram_left: float32 [2, 128, 512, 512], P('section', ('dp', 'mp')), as said below
- gram_right: float32 [2, 128, 512, 512], P('section', ('dp', 'mp')), as said below
- root_left: bfloat16 [2, 128, 512, 512], P('section', ('dp', 'mp'))
- root_right: bfloat16 [2, 128, 512, 512], P('section', ('dp', 'mp'))
- owner_slot: int32 [2, 16, 8], replicated, may hold values from 0 to 127, as said below
- eighth: int32 [2, 16, 8], replicated, may hold values from 0 to 7, as said below
- refresh_phase: int32 [1], replicated, may hold values from 0 to 999999
Outputs:
- new_gram_left: float32 [2, 128, 512, 512], P('section', ('dp', 'mp'))
- new_gram_right: float32 [2, 128, 512, 512], P('section', ('dp', 'mp'))
- new_root_left: bfloat16 [2, 128, 512, 512], P('section', ('dp', 'mp'))
- new_root_right: bfloat16 [2, 128, 512, 512], P('section', ('dp', 'mp'))
- update_blocks: bfloat16 [2, 128, 512, 512], P('section', ('dp', 'mp'))
The draws below stay inside these ranges and needn't reach their ends.
Inputs may be any that keep to these rules, and one draw needn't show every extreme that they name: `owner_slot`: for each section, a permutation of the 128 slots; the block of flat index f = i * 8 + j goes to a slot t with (t) % (8) == f // 16. `eighth`: in each section and each run of 16 consecutive flat block indices, every value is taken by exactly 2 blocks. `gram_left`: symmetric positive definite. `gram_right`: symmetric positive definite.
All inputs are finite; a program needn't handle non-finite values.
Results may differ from the reference program's by a relative error of at most 0.025.
Values may be sent and summed in bfloat16 or wider, within the bound.
No kernel may reach another device: no remote copies, remote signals or barrier semaphores. Data moves between devices by JAX's collectives and lax.ppermute only.
A program may use at most 128 MiB of HBM per device.

```python
import math
import jax
import jax.numpy as jnp
from jax import lax

D = 4096
FFW = 8192
BLK = 512
MB = 2
TOK_MB = 64
ITERS = 2
TOKENS_MB = 1024
NROW = 16
NCOL = 8
SLOTS = 128
GROUP = 16
BPD = 1
N_SECTION = 2
N_DP = 16
N_MP = 8


def gram_draw(key, salt):
    inner_key = jax.random.fold_in(key, salt)
    draw_keys = jax.random.split(inner_key, 8)
    top_count = 3
    support_width = max(BLK // 32, 4)
    batch_count = N_SECTION * SLOTS * top_count
    support_keys = jax.random.split(draw_keys[0], batch_count)
    support = jax.vmap(lambda one_key: jax.random.permutation(one_key, BLK)[:support_width])(support_keys)
    onehot = (support[:, :, None] == jnp.arange(BLK, dtype=jnp.int32)[None, None, :]).astype(jnp.float32)
    sign_values = jnp.where(jax.random.bernoulli(draw_keys[1], 0.5, (batch_count, support_width)), 1.0, -1.0).astype(jnp.float32)
    magnitudes = jax.random.uniform(draw_keys[2], (batch_count, support_width), jnp.float32, 0.5, 1.5)
    ratios = jax.random.uniform(draw_keys[3], (N_SECTION, SLOTS, top_count - 1), jnp.float32, 0.3, 0.6)
    top_level = 40.0 * jax.random.uniform(draw_keys[4], (N_SECTION, SLOTS, 1), jnp.float32, 0.8, 1.2)
    factor = jax.random.uniform(draw_keys[5], (N_SECTION, SLOTS, BLK, BLK), jnp.float32, -1.0, 1.0) * math.sqrt(3.0)
    tail_decay = jnp.power(10.0, -3.0 * jax.random.uniform(draw_keys[6], (N_SECTION, SLOTS, BLK), jnp.float32))
    diagonal = jax.random.uniform(draw_keys[7], (N_SECTION, SLOTS, BLK), jnp.float32, 0.05, 0.2)
    entries = sign_values * magnitudes
    vectors = jnp.einsum('bw,bwn->bn', entries, onehot)
    vectors = vectors / jnp.sqrt(jnp.sum(vectors * vectors, axis=-1, keepdims=True))
    vectors = vectors.reshape(N_SECTION, SLOTS, top_count, BLK)
    strengths = top_level * jnp.concatenate([jnp.ones((N_SECTION, SLOTS, 1), jnp.float32), ratios], axis=-1)
    top_part = jnp.einsum('sbk,sbki,sbkj->sbij', strengths, vectors, vectors)
    tail_part = jnp.einsum('sbij,sbj,sbkj->sbik', factor, tail_decay, factor) / BLK
    matrix = top_part + tail_part + diagonal[..., None] * jnp.eye(BLK, dtype=jnp.float32)
    return 0.5 * (matrix + jnp.swapaxes(matrix, -1, -2))


def root_draw(key, salt):
    inner_key = jax.random.fold_in(key, salt)
    key_diag, key_noise = jax.random.split(inner_key, 2)
    diagonal = jax.random.uniform(key_diag, (N_SECTION, SLOTS, BLK), jnp.float32, 0.3, 0.8)
    noise_part = 0.01 * jax.random.normal(key_noise, (N_SECTION, SLOTS, BLK, BLK), jnp.float32)
    matrix = noise_part + diagonal[..., None] * jnp.eye(BLK, dtype=jnp.float32)
    return matrix.astype(jnp.bfloat16)


def group_shuffles(key, salt):
    group_keys = jax.random.split(jax.random.fold_in(key, salt), N_SECTION * N_MP)
    shuffles = jax.vmap(lambda one_key: jax.random.permutation(one_key, GROUP))(group_keys)
    return shuffles.reshape(N_SECTION, N_MP, GROUP).astype(jnp.int32)


def draw_gram_left(key, part):
    return gram_draw(key, 11)


def draw_gram_right(key, part):
    return gram_draw(key, 12)


def draw_root_left(key, part):
    return root_draw(key, 13)


def draw_root_right(key, part):
    return root_draw(key, 14)


def draw_owner_slot(key, part):
    shuffles = group_shuffles(key, 21)
    group_ids = jnp.arange(N_MP, dtype=jnp.int32)[None, :, None]
    slot_values = (shuffles // BPD * N_MP + group_ids) * BPD + shuffles % BPD
    return slot_values.reshape(N_SECTION, NROW, NCOL).astype(jnp.int32)


def draw_eighth(key, part):
    shuffles = group_shuffles(key, 22)
    return (shuffles % 8).reshape(N_SECTION, NROW, NCOL).astype(jnp.int32)


def block_levels(rng, extent, pieces, low, largest):
    factor_of, own = 1.0, jax.random.fold_in(rng, 6)
    for axis_at, blocks in pieces:
        steps = jnp.exp(jax.random.uniform(jax.random.fold_in(own, axis_at), (blocks,), jnp.float32, low / len(pieces), largest / len(pieces)))
        factor_of = factor_of * jnp.repeat(steps, extent[axis_at] // blocks).reshape([-1 if axis == axis_at else 1 for axis in range(len(extent))])
    return factor_of


def noise(rng, dims, scale, reach, cuts=(), kind=jnp.bfloat16):
    result = jax.random.normal(rng, dims, jnp.float32) * scale
    if len(cuts) > 0:
        result = block_levels(rng, dims, cuts, -0.22, 0.18) * result
    return jnp.clip(result, min=-reach, max=reach).astype(kind)


def setup_inputs(seed: int = 0) -> dict:
    key_of = jax.random.split(jax.random.key(seed), 13)
    activations = noise(key_of[0], (MB, TOKENS_MB, D), 1.0, 6.0, ((1, 16),))
    cotangent = noise(key_of[1], (MB, TOKENS_MB, D), 1.0, 6.0, ((1, 16),))
    norm_gain = jnp.clip(1.0 + 0.18 * jax.random.normal(key_of[2], (N_SECTION, D), jnp.float32), 0.1, 1.9)
    w_up = noise(key_of[3], (N_SECTION, D, FFW), D ** -0.5, 0.09375, ((0, 2), (1, 16), (2, 8)))
    w_down = noise(key_of[4], (N_SECTION, D, FFW), FFW ** -0.5, 0.0625, ((0, 2), (1, 16), (2, 8)))
    gram_left = draw_gram_left(jax.random.fold_in(key_of[12], 71), 0)
    gram_right = draw_gram_right(jax.random.fold_in(key_of[12], 71), 0)
    root_left = draw_root_left(jax.random.fold_in(key_of[12], 71), 0)
    root_right = draw_root_right(jax.random.fold_in(key_of[12], 71), 0)
    owner_slot = draw_owner_slot(jax.random.fold_in(key_of[12], 71), 0)
    eighth = draw_eighth(jax.random.fold_in(key_of[12], 71), 0)
    refresh_phase = jax.random.randint(key_of[11], (1,), 0, 1000000).astype(jnp.int32)
    return {"activations": activations, "cotangent": cotangent, "norm_gain": norm_gain, "w_up": w_up, "w_down": w_down, "gram_left": gram_left, "gram_right": gram_right, "root_left": root_left, "root_right": root_right, "owner_slot": owner_slot, "eighth": eighth, "refresh_phase": refresh_phase}


norm_epsilon = 1e-05
decay_rate = 0.9
ridge_shift = 0.001
highest = lax.Precision.HIGHEST

def normalize_values(values, gain_row):
    inverse_rms = lax.rsqrt(lax.optimization_barrier(jnp.mean(values * values, axis=-1, keepdims=True)) + norm_epsilon)
    return values * inverse_rms * gain_row

def silu_slope(pre_act):
    sigmoid_values = jax.nn.sigmoid(pre_act)
    return sigmoid_values * (1.0 + pre_act * (1.0 - sigmoid_values))

def inverse_root(matrix):
    matrix_order = matrix.shape[-1]
    identity = jnp.eye(matrix_order, dtype=jnp.float32)
    shifted = matrix + ridge_shift * identity
    factor = 2.5 / jnp.sqrt(jnp.sum(shifted * shifted))
    iterate = jnp.power(factor, 0.25) * identity
    moment = factor * shifted
    for sweep_no in range(ITERS):
        step_mat = 1.25 * identity - 0.25 * moment
        square = jnp.dot(step_mat, step_mat, precision=highest)
        fourth = jnp.dot(square, square, precision=highest)
        moment = jnp.dot(fourth, moment, precision=highest)
        iterate = jnp.dot(iterate, step_mat, precision=highest)
    return iterate

def split_sum(left_rows, right_rows):
    left_parts = jnp.moveaxis(left_rows.reshape(left_rows.shape[0], N_MP, -1), 1, 0)
    right_parts = jnp.moveaxis(right_rows.reshape(right_rows.shape[0], N_MP, -1), 1, 0)

    def add_part(running_total, pair_in):
        product = lax.dot_general(pair_in[0], pair_in[1], (((1,), (1,)), ((), ())), preferred_element_type=jnp.float32)
        rounded = lax.optimization_barrier(product.astype(jnp.bfloat16)).astype(jnp.float32)
        return (running_total + rounded, None)
    zero_sum = jnp.zeros((left_rows.shape[0], right_rows.shape[0]), jnp.float32)
    running_total, unused = lax.scan(add_part, zero_sum, (left_parts, right_parts))
    return running_total

def forward_layer(inputs, gain_row, up_rows, down_rows):
    values = inputs.astype(jnp.float32)
    normed = normalize_values(values, gain_row).astype(jnp.bfloat16)
    pre_act = jnp.dot(normed, up_rows, preferred_element_type=jnp.float32)
    hidden = jax.nn.silu(pre_act).astype(jnp.bfloat16)
    output = (values + split_sum(hidden, down_rows)).astype(jnp.bfloat16)
    return (output, pre_act, hidden)

def backward_layer(grad_output, inputs, pre_act, gain_row, up_rows, down_rows):
    grad_hidden = jnp.dot(grad_output, down_rows, preferred_element_type=jnp.float32)
    grad_pre = (grad_hidden * silu_slope(pre_act)).astype(jnp.bfloat16)
    grad_normed = split_sum(grad_pre, up_rows)
    values = inputs.astype(jnp.float32)
    unused, pullback = jax.vjp(lambda values_in: normalize_values(values_in, gain_row), values)
    grad_values = pullback(grad_normed)[0]
    return (grad_output.astype(jnp.float32) + grad_values).astype(jnp.bfloat16)

def reference(activations, cotangent, norm_gain, w_up, w_down, gram_left, gram_right, root_left, root_right, owner_slot, eighth, refresh_phase):
    section_total = w_up.shape[0]
    micro_count, token_rows, model_width = activations.shape
    flat_rows = micro_count * token_rows
    layer_in = activations.reshape(flat_rows, model_width)
    section_saved = []
    for section_no in range(section_total):
        output, pre_act, hidden = forward_layer(layer_in, norm_gain[section_no], w_up[section_no], w_down[section_no])
        section_saved.append((layer_in, pre_act, hidden))
        layer_in = output
    grad_output = cotangent.reshape(flat_rows, model_width)
    section_grads = [None] * section_total
    for section_no in reversed(range(section_total)):
        inputs, pre_act, hidden = section_saved[section_no]
        section_grads[section_no] = (hidden, grad_output)
        if section_no > 0:
            grad_output = backward_layer(grad_output, inputs, pre_act, norm_gain[section_no], w_up[section_no], w_down[section_no])
    phase_now = refresh_phase[0] % 8
    gram_lefts, gram_rights, root_lefts, root_rights, updates = ([], [], [], [], [])
    for section_no in range(section_total):
        hidden, grad_out = section_grads[section_no]
        hidden_rep = hidden.reshape(micro_count, N_DP, TOK_MB, FFW).transpose(1, 0, 2, 3).reshape(N_DP, micro_count * TOK_MB, FFW)
        grad_rep = grad_out.reshape(micro_count, N_DP, TOK_MB, model_width).transpose(1, 0, 2, 3).reshape(N_DP, micro_count * TOK_MB, model_width)

        def add_replica(running_total, pair_in):
            product = lax.dot_general(pair_in[0], pair_in[1], (((0,), (0,)), ((), ())), preferred_element_type=jnp.float32)
            rounded = lax.optimization_barrier(product.astype(jnp.bfloat16)).astype(jnp.float32)
            return (running_total + rounded, None)
        zero_sum = jnp.zeros((FFW, model_width), jnp.float32)
        summed, unused = lax.scan(add_replica, zero_sum, (hidden_rep, grad_rep))
        scaled = summed * (1.0 / math.sqrt(micro_count * token_rows))
        blocks = scaled.reshape(NROW, BLK, NCOL, BLK).transpose(0, 2, 1, 3).reshape(SLOTS, BLK, BLK)
        block_of_slot = jnp.argsort(owner_slot[section_no].reshape(-1)).astype(jnp.int32)
        slot_grad = blocks[block_of_slot]
        is_due = eighth[section_no].reshape(-1)[block_of_slot] == phase_now
        left_new = decay_rate * gram_left[section_no] + jnp.einsum('sij,skj->sik', slot_grad, slot_grad, precision=highest) / BLK
        right_new = decay_rate * gram_right[section_no] + jnp.einsum('sji,sjk->sik', slot_grad, slot_grad, precision=highest) / BLK
        due_slots = jnp.argsort(jnp.logical_not(is_due).astype(jnp.int32), stable=True)[:SLOTS // 8].astype(jnp.int32)
        fresh_left = jax.vmap(inverse_root)(left_new[due_slots]).astype(jnp.bfloat16)
        fresh_right = jax.vmap(inverse_root)(right_new[due_slots]).astype(jnp.bfloat16)
        roots_l = root_left[section_no].at[due_slots].set(fresh_left)
        roots_r = root_right[section_no].at[due_slots].set(fresh_right)
        grad_low = slot_grad.astype(jnp.bfloat16)
        inner_product = jnp.einsum('sij,sjk->sik', grad_low.astype(jnp.float32), roots_r.astype(jnp.float32), precision=highest).astype(jnp.bfloat16)
        update = jnp.einsum('sij,sjk->sik', roots_l.astype(jnp.float32), inner_product.astype(jnp.float32), precision=highest).astype(jnp.bfloat16)
        gram_lefts.append(left_new)
        gram_rights.append(right_new)
        root_lefts.append(roots_l)
        root_rights.append(roots_r)
        updates.append(update)
    return (jnp.stack(gram_lefts), jnp.stack(gram_rights), jnp.stack(root_lefts), jnp.stack(root_rights), jnp.stack(updates))
```

```python
import functools
import math

import jax
import jax.numpy as jnp
from jax import lax
from jax.experimental import pallas as pl
from jax.experimental.pallas import tpu as pltpu
from jax.sharding import PartitionSpec as P

BLK = 512
ITERS = 2

norm_epsilon = 1e-05
decay_rate = 0.9
ridge_shift = 0.001
f32 = jnp.float32
bf16 = jnp.bfloat16


def normalize_values(values, gain_row):
    inverse_rms = lax.rsqrt(jnp.mean(values * values, axis=-1, keepdims=True) + norm_epsilon)
    return values * inverse_rms * gain_row


def silu_slope(pre_act):
    sigmoid_values = jax.nn.sigmoid(pre_act)
    return sigmoid_values * (1.0 + pre_act * (1.0 - sigmoid_values))


def dot(a, b, dims=((1,), (0,))):
    return lax.dot_general(a, b, (dims, ((), ())), preferred_element_type=f32)


def early_kernel(block_cols, info_ref, hidden_ref, cot_ref, o_ref):
    slots = o_ref.shape[0]

    @pl.when(info_ref[0] == 0)
    def _():
        for t in range(slots):
            at = pl.multiple_of((info_ref[2 + t] // block_cols) * BLK, BLK)
            o_ref[t] = hidden_ref[:, pl.ds(at, BLK)]

    @pl.when(info_ref[0] != 0)
    def _():
        for t in range(slots):
            at = pl.multiple_of((info_ref[2 + t] % block_cols) * BLK, BLK)
            o_ref[t] = cot_ref[:, pl.ds(at, BLK)]


def late_kernel(block_cols, info_ref, hidden_ref, *refs):
    chunks, o_ref = refs[:-1], refs[-1]
    slots = o_ref.shape[0]
    count, share = len(chunks), chunks[0].shape[0]

    @pl.when(info_ref[0] == 0)
    def _():
        for k in range(count):
            place = pl.multiple_of(((info_ref[1] + count - k) % count) * share, share)
            for t in range(slots):
                at = pl.multiple_of((info_ref[2 + t] % block_cols) * BLK, BLK)
                o_ref[t, pl.ds(place, share), :] = chunks[k][:, pl.ds(at, BLK)]

    @pl.when(info_ref[0] != 0)
    def _():
        for t in range(slots):
            at = pl.multiple_of((info_ref[2 + t] // block_cols) * BLK, BLK)
            o_ref[t] = hidden_ref[:, pl.ds(at, BLK)]


def place_kernel(info_ref, *refs):
    chunks, o_ref = refs[:-1], refs[-1]
    count, share = len(chunks), chunks[0].shape[0]
    for k in range(count):
        place = pl.multiple_of(((info_ref[1] + count - k) % count) * share, share)
        o_ref[pl.ds(place, share), :] = chunks[k][...]


def whole(kernel, name, shape, info, *arrays):
    vmem = pl.BlockSpec(memory_space=pltpu.VMEM)
    return pl.pallas_call(
        kernel,
        in_specs=[pl.BlockSpec(memory_space=pltpu.SMEM)] + [vmem] * len(arrays),
        out_specs=vmem,
        out_shape=jax.ShapeDtypeStruct(shape, bf16),
        compiler_params=pltpu.CompilerParams(vmem_limit_bytes=40 * 1024 * 1024),
        name=name,
    )(info, *arrays)


def inverse_root(matrix):
    order = matrix.shape[-1]
    row = lax.broadcasted_iota(jnp.int32, (order, order), 0)
    col = lax.broadcasted_iota(jnp.int32, (order, order), 1)
    diag = row == col
    shifted = matrix + jnp.where(diag, ridge_shift, 0.0)
    factor = 2.5 / jnp.sqrt(jnp.sum(shifted * shifted))
    moment = factor * shifted
    step = jnp.where(diag, 1.25, 0.0) - 0.25 * moment
    low = step.astype(bf16)
    square = dot(low, low).astype(bf16)
    fourth = dot(square, square).astype(bf16)
    moment = dot(fourth, moment.astype(bf16))
    last = jnp.where(diag, 1.25, 0.0) - 0.25 * moment
    root = jnp.sqrt(jnp.sqrt(factor))
    return root * dot(low, last.astype(bf16))


def owner_kernel(scale, info_ref, early_ref, late_ref, gl_ref, gr_ref, rl_ref, rr_ref,
                 ngl_ref, ngr_ref, nrl_ref, nrr_ref, up_ref, grad_ref):
    @pl.when(info_ref[0] == 0)
    def _():
        grad_ref[...] = dot(early_ref[...], late_ref[...], ((0,), (0,))) * scale

    @pl.when(info_ref[0] != 0)
    def _():
        grad_ref[...] = dot(late_ref[...], early_ref[...], ((0,), (0,))) * scale

    grad = grad_ref[...]
    low = grad.astype(bf16)
    ngl_ref[...] = decay_rate * gl_ref[...] + dot(low, low, ((1,), (1,))) * (1.0 / BLK)
    ngr_ref[...] = decay_rate * gr_ref[...] + dot(low, low, ((0,), (0,))) * (1.0 / BLK)
    nrl_ref[...] = rl_ref[...]
    nrr_ref[...] = rr_ref[...]

    @pl.when(info_ref[1] == 1)
    def _():
        nrl_ref[...] = inverse_root(ngl_ref[...]).astype(bf16)
        nrr_ref[...] = inverse_root(ngr_ref[...]).astype(bf16)

    right = dot(low, nrr_ref[...]).astype(bf16)
    up_ref[...] = dot(nrl_ref[...], right).astype(bf16)


def owner_step(scale, info, early, late, gram_l, gram_r, root_l, root_r):
    vmem = pl.BlockSpec(memory_space=pltpu.VMEM)
    big = jax.ShapeDtypeStruct((BLK, BLK), f32)
    small = jax.ShapeDtypeStruct((BLK, BLK), bf16)
    return pl.pallas_call(
        functools.partial(owner_kernel, scale),
        in_specs=[pl.BlockSpec(memory_space=pltpu.SMEM)] + [vmem] * 6,
        out_specs=[vmem] * 5,
        out_shape=[big, big, small, small, small],
        scratch_shapes=[pltpu.VMEM((BLK, BLK), f32)],
        compiler_params=pltpu.CompilerParams(vmem_limit_bytes=40 * 1024 * 1024),
        name="owner_step",
    )(info, early, late, gram_l, gram_r, root_l, root_r)


def on_device(
    activations,
    cotangent,
    norm_gain,
    w_up,
    w_down,
    gram_left,
    gram_right,
    root_left,
    root_right,
    owner_slot,
    eighth,
    refresh_phase,
):
    section_no = lax.axis_index("section")
    dp_no = lax.axis_index("dp")
    mp_no = lax.axis_index("mp")
    core = dp_no % 2
    dp_count = lax.axis_size("dp")
    mp_count = lax.axis_size("mp")
    micro_count, row_count, width = activations.shape
    tokens = micro_count * row_count
    share = tokens // mp_count
    chips = dp_count // 2
    depth, shard_ff = w_up.shape[1:]
    half = shard_ff // 2
    gain_row = norm_gain[0]
    is_first = section_no == 0
    on_low_core = core == 0
    same_core = [[2 * q + c for q in range(chips)] for c in range(2)]
    swap_cores = [(i, i ^ 1) for i in range(dp_count)]

    first = jnp.where(is_first, w_up[0], w_down[0])
    second = jnp.where(is_first, w_down[0], w_up[0])
    second_full = lax.all_gather(second, "dp", axis=0, tiled=True)

    act = activations.reshape(tokens, width)
    cot = cotangent.reshape(tokens, width)
    normed = normalize_values(act.astype(f32), gain_row).astype(bf16)
    operand = jnp.where(is_first, normed, cot)

    kept = jnp.where(on_low_core, first[:, :half], first[:, half:])
    given = jnp.where(on_low_core, first[:, half:], first[:, :half])
    taken = lax.ppermute(given, "dp", swap_cores)
    chip_rows = jnp.concatenate(
        [jnp.where(on_low_core, kept, taken), jnp.where(on_low_core, taken, kept)], axis=0
    )

    cut = operand.reshape(tokens, chips, 2 * depth).transpose(1, 0, 2)
    own = lax.all_to_all(
        cut, "dp", split_axis=0, concat_axis=0, axis_index_groups=same_core, tiled=True
    )
    other = lax.ppermute(own, "dp", swap_cores)
    own_product = dot(own.reshape(chips * tokens, 2 * depth), chip_rows).astype(bf16)
    other_product = dot(other.reshape(chips * tokens, 2 * depth), chip_rows).astype(bf16)
    own_product = own_product.reshape(chips, 1, tokens, half)
    other_product = other_product.reshape(chips, 1, tokens, half)
    to_replicas = jnp.concatenate(
        [
            jnp.where(on_low_core, own_product, other_product),
            jnp.where(on_low_core, other_product, own_product),
        ],
        axis=1,
    ).reshape(dp_count, tokens, half)
    parts = lax.all_to_all(to_replicas, "dp", split_axis=0, concat_axis=0, tiled=True)
    halves = jnp.sum(parts.reshape(chips, 2, tokens, half).astype(f32), axis=0)
    product = jnp.concatenate([halves[0], halves[1]], axis=1)
    hidden_first = jax.nn.silu(product).astype(bf16)

    def sum_over_mp(partial_value):
        pieces = lax.all_to_all(
            partial_value.reshape(mp_count, share, width), "mp",
            split_axis=0, concat_axis=0, tiled=True,
        )
        return jnp.sum(pieces.astype(f32), axis=0)

    def ring_over_mp(rows):
        right = [(i, (i + 1) % mp_count) for i in range(mp_count)]
        left = [((i + 1) % mp_count, i) for i in range(mp_count)]
        behind, ahead = [rows], []
        for step in range(mp_count // 2):
            behind.append(lax.ppermute(behind[-1], "mp", right))
            if step < mp_count // 2 - 1:
                ahead.append(lax.ppermute(ahead[-1] if ahead else rows, "mp", left))
        return behind + ahead[::-1]

    block_rows = shard_ff // BLK
    block_cols = width // BLK
    group_size = block_rows * block_cols
    section_owner = lax.dynamic_index_in_dim(owner_slot, section_no, 0, keepdims=False)
    local_owner = lax.dynamic_slice_in_dim(
        section_owner, mp_no * block_rows, block_rows, 0
    ).reshape(-1)
    local_slot = local_owner // mp_count
    slots = jnp.arange(group_size, dtype=jnp.int32)
    block_of_slot = jnp.sum(
        jnp.where(local_slot[None, :] == slots[:, None], slots[None, :], 0), axis=1
    )
    info = jnp.concatenate([jnp.stack([section_no, mp_no]).astype(jnp.int32), block_of_slot])

    def to_owners(blocks):
        return lax.all_to_all(blocks, "dp", split_axis=0, concat_axis=0, tiled=True)

    slot_shape = (group_size, tokens, BLK)
    early_blocks = whole(
        functools.partial(early_kernel, block_cols), "early_blocks", slot_shape, info, hidden_first, cot
    )

    partial_out = dot(hidden_first, second_full, ((1,), (1,))).astype(bf16)
    my_rows = functools.partial(
        lax.dynamic_slice_in_dim, start_index=mp_no * share, slice_size=share, axis=0
    )
    output = (my_rows(act).astype(f32) + sum_over_mp(partial_out)).astype(bf16)
    layer_in = lax.ppermute(output, "section", [(0, 1)])
    early_blocks, layer_in = lax.optimization_barrier((early_blocks, layer_in))
    early = to_owners(early_blocks)
    values = layer_in.astype(f32)
    normed_rows, pullback = jax.vjp(lambda v: normalize_values(v, gain_row), values)
    chunks = ring_over_mp(normed_rows.astype(bf16))
    normed_second = whole(place_kernel, "place", (tokens, width), info, *chunks)
    normed_second, early = lax.optimization_barrier((normed_second, early))
    pre_act = dot(normed_second, second_full)
    hidden_second = jax.nn.silu(pre_act).astype(bf16)

    grad_pre = (product * silu_slope(pre_act)).astype(bf16)
    partial_grad = dot(grad_pre, second_full, ((1,), (1,))).astype(bf16)
    grad_normed = sum_over_mp(partial_grad)
    grad_in = (my_rows(cot).astype(f32) + pullback(grad_normed)[0]).astype(bf16)
    grad_out = lax.ppermute(grad_in, "section", [(1, 0)])
    chunks = ring_over_mp(grad_out)
    late_blocks = whole(
        functools.partial(late_kernel, block_cols), "late_blocks", slot_shape, info,
        hidden_second, *chunks,
    )
    late = to_owners(late_blocks)

    section_eighth = lax.dynamic_index_in_dim(eighth, section_no, 0, keepdims=False)
    local_eighth = lax.dynamic_slice_in_dim(
        section_eighth, mp_no * block_rows, block_rows, 0
    ).reshape(-1)
    my_eighth = jnp.sum(jnp.where(local_slot == dp_no, local_eighth, 0))
    due = (my_eighth == refresh_phase[0] % 8).astype(jnp.int32)
    outs = owner_step(
        1.0 / math.sqrt(tokens * dp_count), jnp.stack([section_no.astype(jnp.int32), due]),
        early.reshape(dp_count * tokens, BLK), late.reshape(dp_count * tokens, BLK),
        gram_left[0, 0], gram_right[0, 0], root_left[0, 0], root_right[0, 0],
    )
    return tuple(o[None, None] for o in outs)


def solution(mesh):
    spread = P("section", ("dp", "mp"), None, None)
    return jax.shard_map(
        on_device,
        mesh=mesh,
        in_specs=(
            P(None, "dp", None),
            P(None, "dp", None),
            P("section", None),
            P("section", "dp", "mp"),
            P("section", "dp", "mp"),
            spread,
            spread,
            spread,
            spread,
            P(),
            P(),
            P(),
        ),
        out_specs=(spread,) * 5,
        check_vma=False,
    )
```

```python
import functools
import math

import jax
import jax.numpy as jnp
from jax import lax
from jax.experimental import pallas as pl
from jax.experimental.pallas import tpu as pltpu
from jax.sharding import PartitionSpec as P

BLK = 512
VMEM = 24 * 1024 * 1024

norm_epsilon = 1e-05
decay_rate = 0.9
ridge_shift = 0.001
f32 = jnp.float32
bf16 = jnp.bfloat16


def normalize_values(values, gain_row):
    inverse_rms = lax.rsqrt(jnp.mean(values * values, axis=-1, keepdims=True) + norm_epsilon)
    return values * inverse_rms * gain_row


def silu_slope(pre_act):
    sigmoid_values = jax.nn.sigmoid(pre_act)
    return sigmoid_values * (1.0 + pre_act * (1.0 - sigmoid_values))


def dot(a, b, dims=((1,), (0,))):
    return lax.dot_general(a, b, (dims, ((), ())), preferred_element_type=f32)


def operand_kernel(where_ref, act_ref, cot_ref, gain_ref, o_ref, held_ref, sem):
    wide = o_ref.shape[2]
    mine = pl.ds(pl.multiple_of(where_ref[1] * wide, wide), wide)
    others = pl.ds(pl.multiple_of((1 - where_ref[1]) * wide, wide), wide)

    @pl.when(where_ref[0] == 0)
    def _():
        copy = pltpu.make_async_copy(act_ref, held_ref, sem)
        copy.start()
        copy.wait()
        normed = normalize_values(held_ref[...].astype(f32), gain_ref[...])
        held_ref[...] = normed.astype(bf16)

    @pl.when(where_ref[0] != 0)
    def _():
        copy = pltpu.make_async_copy(cot_ref, held_ref, sem)
        copy.start()
        copy.wait()

    o_ref[0] = held_ref[:, mine]
    o_ref[1] = held_ref[:, others]


def operand_step(places, act, cot, gain_row):
    tokens, width = act.shape
    vmem = pl.BlockSpec(memory_space=pltpu.VMEM)
    away = pl.BlockSpec(memory_space=pl.ANY)
    return pl.pallas_call(
        operand_kernel,
        in_specs=[pl.BlockSpec(memory_space=pltpu.SMEM), away, away, vmem],
        out_specs=vmem,
        out_shape=jax.ShapeDtypeStruct((2, tokens, width // 2), bf16),
        scratch_shapes=[pltpu.VMEM((tokens, width), bf16), pltpu.SemaphoreType.DMA],
        compiler_params=pltpu.CompilerParams(vmem_limit_bytes=VMEM),
        name="operand",
    )(places, act, cot, gain_row)


def product_kernel(line, where_ref, *refs):
    operands, weights, o_ref = refs[:4], refs[4:-1], refs[-1]
    core, x = where_ref[2], where_ref[3]
    depth = weights[0].shape[0] // 2
    own, behind, far_own, far_other, ahead = weights
    pieces = (
        (0, 0, own, 0), (0, 1, own, depth), (1, 0, behind, 0), (1, 1, behind, depth),
        (2, 0, far_own, 0), (2, 1, far_other, 0), (3, 0, ahead, 0), (3, 1, ahead, depth),
    )
    for g, ref in enumerate(operands):
        total = None
        for k, o, w_ref, down in pieces:
            chip, c = (x + line - k) % line, (core, 1 - core)[o]
            at = pl.multiple_of((2 * chip + c) * depth, depth)
            term = dot(ref[:, pl.ds(at, depth)], w_ref[down : down + depth, :])
            total = term if total is None else total + term
        o_ref[g] = total.astype(bf16)


def whole(kernel, name, shape, numbers, *arrays):
    vmem = pl.BlockSpec(memory_space=pltpu.VMEM)
    return pl.pallas_call(
        kernel,
        in_specs=[pl.BlockSpec(memory_space=pltpu.SMEM)] + [vmem] * len(arrays),
        out_specs=vmem,
        out_shape=jax.ShapeDtypeStruct(shape, bf16),
        compiler_params=pltpu.CompilerParams(vmem_limit_bytes=VMEM),
        name=name,
    )(numbers, *arrays)


def sigmoid(v):
    return 1.0 / (1.0 + jnp.exp(-v))


def rows_of(w_ref, e):
    part = w_ref[:, e]
    return part.reshape(part.shape[0] * part.shape[1], part.shape[2])


def forward_kernel(where_ref, mine_ref, theirs_ref, away_ref, keep_ref, give_ref, half_ref, w_ref, sems):
    core = where_ref[2]
    groups, tokens, half = mine_ref.shape
    copies = [
        pltpu.make_async_copy(away_ref.at[x], w_ref.at[x], sems.at[x]) for x in range(w_ref.shape[0])
    ]
    for copy in copies:
        copy.start()
    pieces = []
    for g in range(groups):
        total = mine_ref[g].astype(f32) + theirs_ref[(g + 2) % groups].astype(f32)
        hidden = (total * sigmoid(total)).astype(bf16)
        if g < 2:
            half_ref[g] = jnp.where(where_ref[0] == 0, hidden, total.astype(bf16))
        pieces.append(hidden)
    hidden = jnp.concatenate(pieces, axis=0)
    for copy in copies:
        copy.wait()
    line, cores, strips, narrow, _ = w_ref.shape
    wide = line * narrow
    for o, c in enumerate((core, 1 - core)):
        for e in range(0, strips, 2):
            rows = [w_ref[:, o, e + k].reshape(wide, half) for k in range(2)]
            value = dot(hidden, jnp.concatenate(rows, axis=0), ((1,), (1,))).astype(bf16)
            value = value.reshape(groups, tokens, 2 * wide)
            to = pl.ds(pl.multiple_of((c * strips + e) * wide, 2 * wide), 2 * wide)
            keep_ref[0, :, to] = value[0]
            keep_ref[1, :, to] = value[2]
            give_ref[0, :, to] = value[1]
            give_ref[1, :, to] = value[3]


def forward_step(places, mine, theirs, weight):
    groups, tokens, half = mine.shape
    line, cores, strips, narrow, _ = weight.shape
    vmem = pl.BlockSpec(memory_space=pltpu.VMEM)
    wide = jax.ShapeDtypeStruct((2, tokens, line * cores * strips * narrow), bf16)
    return pl.pallas_call(
        forward_kernel,
        in_specs=[
            pl.BlockSpec(memory_space=pltpu.SMEM), vmem, vmem, pl.BlockSpec(memory_space=pl.ANY)
        ],
        out_specs=[vmem] * 3,
        out_shape=[wide, wide, jax.ShapeDtypeStruct((2, tokens, half), bf16)],
        scratch_shapes=[pltpu.VMEM(weight.shape, bf16), pltpu.SemaphoreType.DMA((line,))],
        compiler_params=pltpu.CompilerParams(vmem_limit_bytes=VMEM),
        name="forward_step",
    )(places, mine, theirs, weight)


def join_kernel(where_ref, keep_ref, got_ref, o_ref):
    count, groups, share, _ = o_ref.shape
    for g in range(groups):
        total = (keep_ref[g].astype(f32) + got_ref[g].astype(f32)).astype(bf16)
        for k in range(count):
            o_ref[k, g] = total[k * share : (k + 1) * share, :]


def second_kernel(info_ref, gain_ref, product_ref, w_ref, *refs):
    chunks = refs[:-6]
    hidden_ref, out_ref, normed_ref, pre_ref, held_ref, sems = refs[-6:]
    count, share = len(chunks), chunks[0].shape[0]
    steps, block_cols, strips, narrow, _ = held_ref.shape
    wide = block_cols * narrow

    copies = [
        pltpu.make_async_copy(w_ref.at[:, pl.ds(i * strips, strips)], held_ref.at[i], sems.at[i])
        for i in range(steps)
    ]
    for copy in copies:
        copy.start()
    for k in range(count):
        place = pl.multiple_of(((info_ref[1] + count - k) % count) * share, share)
        normed = normalize_values(chunks[k][...].astype(f32), gain_ref[...])
        normed_ref[pl.ds(place, share), :] = normed.astype(bf16)
    for i in range(steps):
        copies[i].wait()
        total = None if i == 0 else pre_ref[...]
        for e in range(strips):
            at = (i * strips + e) * wide
            rows = held_ref[i, :, e].reshape(wide, held_ref.shape[4])
            term = dot(normed_ref[:, at : at + wide], rows)
            total = term if total is None else total + term
        pre_ref[...] = total
    pre = pre_ref[...]
    gate = sigmoid(pre)
    hidden_ref[...] = (pre * gate).astype(bf16)
    grad = (product_ref[...].astype(f32) * (gate * (1.0 + pre * (1.0 - gate)))).astype(bf16)
    for i in range(steps):
        for e in range(strips):
            at = (i * strips + e) * wide
            rows = held_ref[i, :, e].reshape(wide, held_ref.shape[4])
            out_ref[:, at : at + wide] = dot(grad, rows, ((1,), (1,))).astype(bf16)


def second_step(info, chunks, gain_row, product, weight):
    tokens, ff = product.shape
    block_cols, strips, narrow, _ = weight.shape
    width = strips * block_cols * narrow
    each = 2
    steps = strips // each
    vmem = pl.BlockSpec(memory_space=pltpu.VMEM)
    return pl.pallas_call(
        second_kernel,
        in_specs=[
            pl.BlockSpec(memory_space=pltpu.SMEM), vmem, vmem, pl.BlockSpec(memory_space=pl.ANY)
        ]
        + [vmem] * len(chunks),
        out_specs=[vmem, vmem],
        out_shape=[
            jax.ShapeDtypeStruct((tokens, ff), bf16),
            jax.ShapeDtypeStruct((tokens, width), bf16),
        ],
        scratch_shapes=[
            pltpu.VMEM((tokens, width), bf16),
            pltpu.VMEM((tokens, ff), f32),
            pltpu.VMEM((steps, block_cols, each, narrow, ff), bf16),
            pltpu.SemaphoreType.DMA((steps,)),
        ],
        compiler_params=pltpu.CompilerParams(vmem_limit_bytes=48 * 1024 * 1024),
        name="second_step",
    )(info, gain_row, product, weight, *chunks)


def strip_kernel(scale, block_cols, info_ref, hidden_ref, *refs):
    chunks, (out_ref, total_ref, held_ref, sems) = refs[:-4], refs[-4:]
    count = len(chunks)
    slots, narrow, _ = out_ref.shape
    copies = [
        pltpu.make_async_copy(
            hidden_ref.at[:, lax.rem(info_ref[1] + count - k, count)], held_ref.at[k], sems.at[k]
        )
        for k in range(count)
    ]
    for copy in copies:
        copy.start()
    _, replicas, share, ff = held_ref.shape
    for k in range(count):
        copies[k].wait()
        value = dot(chunks[k][...], held_ref[k].reshape(replicas * share, ff), ((0,), (0,)))
        if k == 0:
            total_ref[...] = value
        else:
            total_ref[...] += value
    for t in range(slots):
        block = info_ref[2 + t]
        down = pl.multiple_of((block % block_cols) * narrow, narrow)
        across = pl.multiple_of((block // block_cols) * BLK, BLK)
        out_ref[t] = (total_ref[pl.ds(down, narrow), pl.ds(across, BLK)] * scale).astype(bf16)


def strip_step(scale, info, hidden_all, chunks, slots):
    replicas, count, share, ff = hidden_all.shape
    wide = chunks[0].shape[1]
    block_cols = slots // (ff // BLK)
    narrow = wide // block_cols
    vmem = pl.BlockSpec(memory_space=pltpu.VMEM)
    return pl.pallas_call(
        functools.partial(strip_kernel, scale, block_cols),
        in_specs=[pl.BlockSpec(memory_space=pltpu.SMEM), pl.BlockSpec(memory_space=pl.ANY)]
        + [vmem] * len(chunks),
        out_specs=vmem,
        out_shape=jax.ShapeDtypeStruct((slots, narrow, BLK), bf16),
        scratch_shapes=[
            pltpu.VMEM((wide, ff), f32),
            pltpu.VMEM((count, replicas, share, ff), bf16),
            pltpu.SemaphoreType.DMA((count,)),
        ],
        compiler_params=pltpu.CompilerParams(vmem_limit_bytes=50 * 1024 * 1024),
        name="strip_step",
    )(info, hidden_all, *chunks)


def inverse_root(matrix):
    order = matrix.shape[-1]
    row = lax.broadcasted_iota(jnp.int32, (order, order), 0)
    col = lax.broadcasted_iota(jnp.int32, (order, order), 1)
    diag = row == col
    shifted = matrix + jnp.where(diag, ridge_shift, 0.0)
    factor = 2.5 / jnp.sqrt(jnp.sum(shifted * shifted))
    moment = factor * shifted
    step = jnp.where(diag, 1.25, 0.0) - 0.25 * moment
    low = step.astype(bf16)
    square = dot(low, low).astype(bf16)
    fourth = dot(square, square).astype(bf16)
    moment = dot(fourth, moment.astype(bf16))
    last = jnp.where(diag, 1.25, 0.0) - 0.25 * moment
    root = jnp.sqrt(jnp.sqrt(factor))
    return root * dot(low, last.astype(bf16))


def owner_kernel(due_ref, grad_ref, gl_ref, gr_ref, rl_ref, rr_ref,
                 ngl_ref, ngr_ref, nrl_ref, nrr_ref, up_ref):
    turned = grad_ref[...]
    ngl_ref[...] = decay_rate * gl_ref[...] + dot(turned, turned, ((0,), (0,))) * (1.0 / BLK)
    ngr_ref[...] = decay_rate * gr_ref[...] + dot(turned, turned, ((1,), (1,))) * (1.0 / BLK)
    nrl_ref[...] = rl_ref[...]
    nrr_ref[...] = rr_ref[...]

    @pl.when(due_ref[0] == 1)
    def _():
        nrl_ref[...] = inverse_root(ngl_ref[...]).astype(bf16)
        nrr_ref[...] = inverse_root(ngr_ref[...]).astype(bf16)

    right = dot(turned, nrr_ref[...], ((0,), (0,))).astype(bf16)
    up_ref[...] = dot(nrl_ref[...], right).astype(bf16)


def owner_step(due, turned, gram_l, gram_r, root_l, root_r):
    vmem = pl.BlockSpec(memory_space=pltpu.VMEM)
    big = jax.ShapeDtypeStruct((BLK, BLK), f32)
    small = jax.ShapeDtypeStruct((BLK, BLK), bf16)
    return pl.pallas_call(
        owner_kernel,
        in_specs=[pl.BlockSpec(memory_space=pltpu.SMEM)] + [vmem] * 5,
        out_specs=[vmem] * 5,
        out_shape=[big, big, small, small, small],
        compiler_params=pltpu.CompilerParams(vmem_limit_bytes=VMEM),
        name="owner_step",
    )(due, turned, gram_l, gram_r, root_l, root_r)


def on_device(
    activations,
    cotangent,
    norm_gain,
    w_up,
    w_down,
    gram_left,
    gram_right,
    root_left,
    root_right,
    owner_slot,
    eighth,
    refresh_phase,
):
    section_no = lax.axis_index("section")
    dp_no = lax.axis_index("dp")
    mp_no = lax.axis_index("mp")
    dp_count = lax.axis_size("dp")
    mp_count = lax.axis_size("mp")
    micro_count, row_count, width = activations.shape
    tokens = micro_count * row_count
    share = tokens // mp_count
    rows, line = 2, dp_count // 4
    row_no, chip_no, core = dp_no // (2 * line), dp_no // 2 % line, dp_no % 2
    depth, shard_ff = w_up.shape[1:]
    half = shard_ff // 2
    gain_row = norm_gain[0]
    is_first = section_no == 0
    on_low_core = core == 0
    on_low_row = row_no == 0
    same_line = [
        [2 * (line * y + x) + c for x in range(line)] for y in range(rows) for c in range(2)
    ]
    swap_cores = [(i, i ^ 1) for i in range(dp_count)]
    swap_rows = [(i, (i + 2 * line) % dp_count) for i in range(dp_count)]

    first = jnp.where(is_first, w_up[0], w_down[0])
    second = jnp.where(is_first, w_down[0], w_up[0])
    both = jnp.stack([first, second])
    kept = jnp.where(on_low_core, both[:, :, :half], both[:, :, half:])
    given = jnp.where(on_low_core, both[:, :, half:], both[:, :, :half])
    taken = lax.ppermute(given, "dp", swap_cores)
    chip_rows = jnp.concatenate([kept, taken], axis=1)
    second_line = lax.all_gather(
        chip_rows[1], "dp", axis=0, axis_index_groups=same_line, tiled=True
    )
    onward, back = [
        [
            (2 * (line * y + x) + c, 2 * (line * y + (x + k) % line) + c)
            for y in range(rows) for x in range(line) for c in range(2)
        ]
        for k in (1, line - 1)
    ]
    behind = lax.ppermute(chip_rows[0], "dp", onward)
    ahead = lax.ppermute(chip_rows[0], "dp", back)
    first_line = [
        chip_rows[0], behind, lax.ppermute(behind[:depth], "dp", onward),
        lax.ppermute(ahead[depth:], "dp", back), ahead,
    ]

    act = activations.reshape(tokens, width)
    cot = cotangent.reshape(tokens, width)
    places = jnp.stack([section_no, row_no, core, chip_no]).astype(jnp.int32)

    operand = operand_step(places, act, cot, gain_row[None])
    row_operand = lax.ppermute(operand[1], "dp", swap_rows)
    core_operand = lax.ppermute(operand[0], "dp", swap_cores)
    far_operand = lax.ppermute(row_operand, "dp", swap_cores)
    mine = whole(
        functools.partial(product_kernel, line), "first_product", (4, tokens, half), places,
        operand[0], core_operand, row_operand, far_operand, *first_line,
    )
    theirs = lax.ppermute(mine, "dp", swap_rows)

    block_rows = shard_ff // BLK
    block_cols = width // BLK
    narrow = BLK // dp_count

    def by_strips(values):
        lead = values.shape[0]
        cut_up = values.reshape(lead, block_cols, dp_count, narrow)
        return cut_up.transpose(0, 2, 1, 3).reshape(lead, width)

    keep, give, halves = forward_step(
        places, mine, theirs, second_line.reshape(line, 2, depth // narrow, narrow, half)
    )
    second, halves = lax.optimization_barrier((second, halves))
    weight = lax.all_gather(second, "dp", axis=0, tiled=True).reshape(
        block_cols, dp_count, narrow, shard_ff
    )
    got = lax.ppermute(give, "dp", swap_cores)
    to_mp = whole(
        join_kernel, "join", (mp_count, 2, share, width // 2), places, keep, got
    )
    other_half = lax.ppermute(halves[1], "dp", swap_cores)
    product = jnp.concatenate(
        [
            jnp.where(on_low_core, halves[0], other_half),
            jnp.where(on_low_core, other_half, halves[0]),
        ],
        axis=1,
    )

    def sum_over_mp(partial_value):
        pieces = lax.all_to_all(
            partial_value, "mp",
            split_axis=0, concat_axis=0, tiled=True,
        )
        return jnp.sum(pieces.astype(f32), axis=0)

    def ring_over_mp(rows):
        right = [(i, (i + 1) % mp_count) for i in range(mp_count)]
        left = [((i + 1) % mp_count, i) for i in range(mp_count)]
        behind, ahead = [rows], []
        for step in range(mp_count // 2):
            behind.append(lax.ppermute(behind[-1], "mp", right))
            if step < mp_count // 2 - 1:
                ahead.append(lax.ppermute(ahead[-1] if ahead else rows, "mp", left))
        return behind + ahead[::-1]

    group_size = block_rows * block_cols
    section_owner = lax.dynamic_index_in_dim(owner_slot, section_no, 0, keepdims=False)
    local_owner = lax.dynamic_slice_in_dim(
        section_owner, mp_no * block_rows, block_rows, 0
    ).reshape(-1)
    local_slot = local_owner // mp_count
    slots = jnp.arange(group_size, dtype=jnp.int32)
    block_of_slot = jnp.sum(
        jnp.where(local_slot[None, :] == slots[:, None], slots[None, :], 0), axis=1
    )
    info = jnp.concatenate([jnp.stack([section_no, mp_no]).astype(jnp.int32), block_of_slot])

    my_rows = functools.partial(
        lax.dynamic_slice_in_dim, start_index=mp_no * share, slice_size=share, axis=0
    )
    to_mp, act, cot, gain_row = lax.optimization_barrier((to_mp, act, cot, gain_row))
    my_act = by_strips(my_rows(act))
    my_cot = by_strips(my_rows(cot))
    gain_strips = by_strips(gain_row[None])
    branch = sum_over_mp(to_mp).astype(bf16)
    straight = lax.ppermute(
        branch[0], ("section", "dp"), [(i, dp_count + i) for i in range(dp_count)]
    )
    crossed = lax.ppermute(
        branch[1], ("section", "dp"), [(i, dp_count + j) for i, j in swap_rows]
    )
    strip_cut = (share, dp_count, 1, width // (2 * dp_count))
    low = jnp.where(on_low_row, straight, crossed).reshape(strip_cut)
    high = jnp.where(on_low_row, crossed, straight).reshape(strip_cut)
    branch_rows = jnp.concatenate([low, high], axis=2).reshape(share, width)
    layer_in = (my_act.astype(f32) + branch_rows.astype(f32)).astype(bf16)
    hidden_second, partial_grad = second_step(
        info, ring_over_mp(layer_in), gain_strips, product, weight
    )
    hidden_all = lax.all_gather(
        jnp.where(is_first, product, hidden_second), "dp", axis=0, tiled=True
    )

    grad_normed = sum_over_mp(partial_grad.reshape(mp_count, share, width))
    unused, pullback = jax.vjp(
        lambda v: normalize_values(v, gain_strips), layer_in.astype(f32)
    )
    grad_in = (my_cot.astype(f32) + pullback(grad_normed)[0]).astype(bf16)

    def strips_of(values):
        return values.reshape(share, dp_count, width // dp_count).transpose(1, 0, 2)

    arrived = lax.all_to_all(
        jnp.concatenate([strips_of(grad_in), strips_of(my_cot)], axis=0), ("section", "dp"),
        split_axis=0, concat_axis=0, tiled=True,
    )
    strip = arrived[dp_count:].reshape(dp_count * share, width // dp_count)
    strips_out = strip_step(
        1.0 / math.sqrt(tokens * dp_count), info,
        hidden_all.reshape(dp_count, mp_count, share, shard_ff), ring_over_mp(strip), group_size,
    )
    turned = lax.all_to_all(strips_out, "dp", split_axis=0, concat_axis=0, tiled=True)

    section_eighth = lax.dynamic_index_in_dim(eighth, section_no, 0, keepdims=False)
    local_eighth = lax.dynamic_slice_in_dim(
        section_eighth, mp_no * block_rows, block_rows, 0
    ).reshape(-1)
    my_eighth = jnp.sum(jnp.where(local_slot == dp_no, local_eighth, 0))
    due = (my_eighth == refresh_phase[0] % 8).astype(jnp.int32)
    outs = owner_step(
        due.reshape(1), turned.reshape(BLK, BLK),
        gram_left[0, 0], gram_right[0, 0], root_left[0, 0], root_right[0, 0],
    )
    return tuple(o[None, None] for o in outs)


def solution(mesh):
    spread = P("section", ("dp", "mp"), None, None)
    return jax.shard_map(
        on_device,
        mesh=mesh,
        in_specs=(
            P(None, "dp", None),
            P(None, "dp", None),
            P("section", None),
            P("section", "dp", "mp"),
            P("section", "dp", "mp"),
            spread,
            spread,
            spread,
            spread,
            P(),
            P(),
            P(),
        ),
        out_specs=(spread,) * 5,
        check_vma=False,
    )
```

```python
import functools
import math

import jax
import jax.numpy as jnp
from jax import lax
from jax.experimental import pallas as pl
from jax.experimental.pallas import tpu as pltpu
from jax.sharding import PartitionSpec as P

BLK = 512
VMEM = 24 * 1024 * 1024

norm_epsilon = 1e-05
decay_rate = 0.9
ridge_shift = 0.001
f32 = jnp.float32
bf16 = jnp.bfloat16


def normalize_values(values, gain_row):
    inverse_rms = lax.rsqrt(jnp.mean(values * values, axis=-1, keepdims=True) + norm_epsilon)
    return values * inverse_rms * gain_row


def silu_slope(pre_act):
    sigmoid_values = jax.nn.sigmoid(pre_act)
    return sigmoid_values * (1.0 + pre_act * (1.0 - sigmoid_values))


def dot(a, b, dims=((1,), (0,))):
    return lax.dot_general(a, b, (dims, ((), ())), preferred_element_type=f32)


def operand_kernel(where_ref, act_ref, cot_ref, gain_ref, o_ref, held_ref, sem):
    wide = o_ref.shape[2]
    mine = pl.ds(pl.multiple_of(where_ref[1] * wide, wide), wide)
    others = pl.ds(pl.multiple_of((1 - where_ref[1]) * wide, wide), wide)

    @pl.when(where_ref[0] == 0)
    def _():
        copy = pltpu.make_async_copy(act_ref, held_ref, sem)
        copy.start()
        copy.wait()
        normed = normalize_values(held_ref[...].astype(f32), gain_ref[...])
        held_ref[...] = normed.astype(bf16)

    @pl.when(where_ref[0] != 0)
    def _():
        copy = pltpu.make_async_copy(cot_ref, held_ref, sem)
        copy.start()
        copy.wait()

    o_ref[0] = held_ref[:, mine]
    o_ref[1] = held_ref[:, others]


def operand_step(places, act, cot, gain_row):
    tokens, width = act.shape
    vmem = pl.BlockSpec(memory_space=pltpu.VMEM)
    away = pl.BlockSpec(memory_space=pltpu.HBM)
    return pl.pallas_call(
        operand_kernel,
        in_specs=[pl.BlockSpec(memory_space=pltpu.SMEM), away, away, vmem],
        out_specs=vmem,
        out_shape=jax.ShapeDtypeStruct((2, tokens, width // 2), bf16),
        scratch_shapes=[pltpu.VMEM((tokens, width), bf16), pltpu.SemaphoreType.DMA],
        compiler_params=pltpu.CompilerParams(vmem_limit_bytes=VMEM),
        name="operand",
    )(places, act, cot, gain_row)


def product_kernel(line, where_ref, *refs):
    operands, weights, o_ref = refs[:4], refs[4:-1], refs[-1]
    core, x = where_ref[2], where_ref[3]
    depth = weights[0].shape[0] // 2
    own, behind, far_own, far_other, ahead = weights
    pieces = (
        (0, 0, own, 0), (0, 1, own, depth), (1, 0, behind, 0), (1, 1, behind, depth),
        (2, 0, far_own, 0), (2, 1, far_other, 0), (3, 0, ahead, 0), (3, 1, ahead, depth),
    )
    for g, ref in enumerate(operands):
        total = None
        for k, o, w_ref, down in pieces:
            chip, c = (x + line - k) % line, (core, 1 - core)[o]
            at = pl.multiple_of((2 * chip + c) * depth, depth)
            term = dot(ref[:, pl.ds(at, depth)], w_ref[down : down + depth, :])
            total = term if total is None else total + term
        o_ref[g] = total.astype(bf16)


def whole(kernel, name, shape, numbers, *arrays):
    vmem = pl.BlockSpec(memory_space=pltpu.VMEM)
    return pl.pallas_call(
        kernel,
        in_specs=[pl.BlockSpec(memory_space=pltpu.SMEM)] + [vmem] * len(arrays),
        out_specs=vmem,
        out_shape=jax.ShapeDtypeStruct(shape, bf16),
        compiler_params=pltpu.CompilerParams(vmem_limit_bytes=VMEM),
        name=name,
    )(numbers, *arrays)


def sigmoid(v):
    return 1.0 / (1.0 + jnp.exp(-v))


def rows_of(w_ref, e):
    part = w_ref[:, e]
    return part.reshape(part.shape[0] * part.shape[1], part.shape[2])


def forward_kernel(where_ref, mine_ref, theirs_ref, away_ref, keep_ref, give_ref, half_ref, w_ref, sems):
    core = where_ref[2]
    groups, tokens, half = mine_ref.shape
    copies = [
        pltpu.make_async_copy(away_ref.at[x], w_ref.at[x], sems.at[x]) for x in range(w_ref.shape[0])
    ]
    for copy in copies:
        copy.start()
    pieces = []
    for g in range(groups):
        total = mine_ref[g].astype(f32) + theirs_ref[(g + 2) % groups].astype(f32)
        hidden = (total * sigmoid(total)).astype(bf16)
        if g < 2:
            half_ref[g] = jnp.where(where_ref[0] == 0, hidden, total.astype(bf16))
        pieces.append(hidden)
    hidden = jnp.concatenate(pieces, axis=0)
    for copy in copies:
        copy.wait()
    line, cores, strips, narrow, _ = w_ref.shape
    wide = line * narrow
    for o, c in enumerate((core, 1 - core)):
        for e in range(0, strips, 2):
            rows = [w_ref[:, o, e + k].reshape(wide, half) for k in range(2)]
            value = dot(hidden, jnp.concatenate(rows, axis=0), ((1,), (1,))).astype(bf16)
            value = value.reshape(groups, tokens, 2 * wide)
            to = pl.ds(pl.multiple_of((c * strips + e) * wide, 2 * wide), 2 * wide)
            keep_ref[0, :, to] = value[0]
            keep_ref[1, :, to] = value[2]
            give_ref[0, :, to] = value[1]
            give_ref[1, :, to] = value[3]


def forward_step(places, mine, theirs, weight):
    groups, tokens, half = mine.shape
    line, cores, strips, narrow, _ = weight.shape
    vmem = pl.BlockSpec(memory_space=pltpu.VMEM)
    wide = jax.ShapeDtypeStruct((2, tokens, line * cores * strips * narrow), bf16)
    return pl.pallas_call(
        forward_kernel,
        in_specs=[
            pl.BlockSpec(memory_space=pltpu.SMEM), vmem, vmem, pl.BlockSpec(memory_space=pltpu.HBM)
        ],
        out_specs=[vmem] * 3,
        out_shape=[wide, wide, jax.ShapeDtypeStruct((2, tokens, half), bf16)],
        scratch_shapes=[pltpu.VMEM(weight.shape, bf16), pltpu.SemaphoreType.DMA((line,))],
        compiler_params=pltpu.CompilerParams(vmem_limit_bytes=VMEM),
        name="forward_step",
    )(places, mine, theirs, weight)


def join_kernel(where_ref, keep_ref, got_ref, o_ref):
    count, groups, share, _ = o_ref.shape
    for g in range(groups):
        total = (keep_ref[g].astype(f32) + got_ref[g].astype(f32)).astype(bf16)
        for k in range(count):
            o_ref[k, g] = total[k * share : (k + 1) * share, :]


def second_kernel(info_ref, gain_ref, product_ref, w_ref, *refs):
    chunks = refs[:-6]
    hidden_ref, out_ref, normed_ref, pre_ref, held_ref, sems = refs[-6:]
    count, share = len(chunks), chunks[0].shape[0]
    steps, block_cols, strips, narrow, _ = held_ref.shape
    wide = block_cols * narrow

    copies = [
        pltpu.make_async_copy(w_ref.at[:, pl.ds(i * strips, strips)], held_ref.at[i], sems.at[i])
        for i in range(steps)
    ]
    for copy in copies:
        copy.start()
    for k in range(count):
        place = pl.multiple_of(((info_ref[1] + count - k) % count) * share, share)
        normed = normalize_values(chunks[k][...].astype(f32), gain_ref[...])
        normed_ref[pl.ds(place, share), :] = normed.astype(bf16)
    for i in range(steps):
        copies[i].wait()
        total = None if i == 0 else pre_ref[...]
        for e in range(strips):
            at = (i * strips + e) * wide
            rows = held_ref[i, :, e].reshape(wide, held_ref.shape[4])
            term = dot(normed_ref[:, at : at + wide], rows)
            total = term if total is None else total + term
        pre_ref[...] = total
    pre = pre_ref[...]
    gate = sigmoid(pre)
    hidden_ref[...] = jnp.where(info_ref[0] == 0, product_ref[...], (pre * gate).astype(bf16))
    grad = (product_ref[...].astype(f32) * (gate * (1.0 + pre * (1.0 - gate)))).astype(bf16)
    for i in range(steps):
        for e in range(strips):
            at = (i * strips + e) * wide
            rows = held_ref[i, :, e].reshape(wide, held_ref.shape[4])
            out_ref[:, at : at + wide] = dot(grad, rows, ((1,), (1,))).astype(bf16)


def second_step(info, chunks, gain_row, product, weight):
    tokens, ff = product.shape
    block_cols, strips, narrow, _ = weight.shape
    width = strips * block_cols * narrow
    each = 2
    steps = strips // each
    vmem = pl.BlockSpec(memory_space=pltpu.VMEM)
    return pl.pallas_call(
        second_kernel,
        in_specs=[
            pl.BlockSpec(memory_space=pltpu.SMEM), vmem, vmem, pl.BlockSpec(memory_space=pltpu.HBM)
        ]
        + [vmem] * len(chunks),
        out_specs=[vmem, vmem],
        out_shape=[
            jax.ShapeDtypeStruct((tokens, ff), bf16),
            jax.ShapeDtypeStruct((tokens, width), bf16),
        ],
        scratch_shapes=[
            pltpu.VMEM((tokens, width), bf16),
            pltpu.VMEM((tokens, ff), f32),
            pltpu.VMEM((steps, block_cols, each, narrow, ff), bf16),
            pltpu.SemaphoreType.DMA((steps,)),
        ],
        compiler_params=pltpu.CompilerParams(vmem_limit_bytes=48 * 1024 * 1024),
        name="second_step",
    )(info, gain_row, product, weight, *chunks)


def strip_kernel(scale, block_cols, info_ref, hidden_ref, *refs):
    chunks, (out_ref, total_ref, held_ref, sems) = refs[:-4], refs[-4:]
    count = len(chunks)
    slots, narrow, _ = out_ref.shape
    copies = [
        pltpu.make_async_copy(
            hidden_ref.at[:, lax.rem(info_ref[1] + count - k, count)], held_ref.at[k], sems.at[k]
        )
        for k in range(count)
    ]
    for copy in copies:
        copy.start()
    _, replicas, share, ff = held_ref.shape
    for k in range(count):
        copies[k].wait()
        value = dot(chunks[k][...], held_ref[k].reshape(replicas * share, ff), ((0,), (0,)))
        if k == 0:
            total_ref[...] = value
        else:
            total_ref[...] += value
    for t in range(slots):
        block = info_ref[2 + t]
        down = pl.multiple_of((block % block_cols) * narrow, narrow)
        across = pl.multiple_of((block // block_cols) * BLK, BLK)
        out_ref[t] = (total_ref[pl.ds(down, narrow), pl.ds(across, BLK)] * scale).astype(bf16)


def strip_step(scale, info, hidden_all, chunks, slots):
    replicas, count, share, ff = hidden_all.shape
    wide = chunks[0].shape[1]
    block_cols = slots // (ff // BLK)
    narrow = wide // block_cols
    vmem = pl.BlockSpec(memory_space=pltpu.VMEM)
    return pl.pallas_call(
        functools.partial(strip_kernel, scale, block_cols),
        in_specs=[pl.BlockSpec(memory_space=pltpu.SMEM), pl.BlockSpec(memory_space=pltpu.HBM)]
        + [vmem] * len(chunks),
        out_specs=vmem,
        out_shape=jax.ShapeDtypeStruct((slots, narrow, BLK), bf16),
        scratch_shapes=[
            pltpu.VMEM((wide, ff), f32),
            pltpu.VMEM((count, replicas, share, ff), bf16),
            pltpu.SemaphoreType.DMA((count,)),
        ],
        compiler_params=pltpu.CompilerParams(vmem_limit_bytes=50 * 1024 * 1024),
        name="strip_step",
    )(info, hidden_all, *chunks)


def inverse_root(matrix):
    order = matrix.shape[-1]
    row = lax.broadcasted_iota(jnp.int32, (order, order), 0)
    col = lax.broadcasted_iota(jnp.int32, (order, order), 1)
    diag = row == col
    shifted = matrix + jnp.where(diag, ridge_shift, 0.0)
    factor = 2.5 / jnp.sqrt(jnp.sum(shifted * shifted))
    moment = factor * shifted
    step = jnp.where(diag, 1.25, 0.0) - 0.25 * moment
    low = step.astype(bf16)
    square = dot(low, low).astype(bf16)
    fourth = dot(square, square).astype(bf16)
    moment = dot(fourth, moment.astype(bf16))
    last = jnp.where(diag, 1.25, 0.0) - 0.25 * moment
    root = jnp.sqrt(jnp.sqrt(factor))
    return root * dot(low, last.astype(bf16))


def owner_kernel(due_ref, grad_ref, gl_away, gr_away, rl_away, rr_away,
                 ngl_ref, ngr_ref, nrl_ref, nrr_ref, up_ref, gl_ref, gr_ref, sems):
    copies = [
        pltpu.make_async_copy(source, target, sems.at[n])
        for n, (source, target) in enumerate(
            ((gl_away, gl_ref), (gr_away, gr_ref), (rr_away, nrr_ref), (rl_away, nrl_ref))
        )
    ]
    for copy in copies:
        copy.start()
    turned = grad_ref[...]
    left = dot(turned, turned, ((0,), (0,))) * (1.0 / BLK)
    copies[0].wait()
    ngl_ref[...] = decay_rate * gl_ref[...] + left
    right = dot(turned, turned, ((1,), (1,))) * (1.0 / BLK)
    copies[1].wait()
    ngr_ref[...] = decay_rate * gr_ref[...] + right
    copies[2].wait()
    copies[3].wait()

    @pl.when(due_ref[0] == 1)
    def _():
        nrl_ref[...] = inverse_root(ngl_ref[...]).astype(bf16)
        nrr_ref[...] = inverse_root(ngr_ref[...]).astype(bf16)

    inner = dot(turned, nrr_ref[...], ((0,), (0,))).astype(bf16)
    up_ref[...] = dot(nrl_ref[...], inner).astype(bf16)


def owner_step(due, turned, gram_l, gram_r, root_l, root_r):
    vmem = pl.BlockSpec(memory_space=pltpu.VMEM)
    away = pl.BlockSpec(memory_space=pltpu.HBM)
    big = jax.ShapeDtypeStruct((BLK, BLK), f32)
    small = jax.ShapeDtypeStruct((BLK, BLK), bf16)
    return pl.pallas_call(
        owner_kernel,
        in_specs=[pl.BlockSpec(memory_space=pltpu.SMEM), vmem] + [away] * 4,
        out_specs=[vmem] * 5,
        out_shape=[big, big, small, small, small],
        scratch_shapes=[
            pltpu.VMEM((BLK, BLK), f32), pltpu.VMEM((BLK, BLK), f32), pltpu.SemaphoreType.DMA((4,))
        ],
        compiler_params=pltpu.CompilerParams(vmem_limit_bytes=VMEM),
        name="owner_step",
    )(due, turned, gram_l, gram_r, root_l, root_r)


def on_device(
    activations,
    cotangent,
    norm_gain,
    w_up,
    w_down,
    gram_left,
    gram_right,
    root_left,
    root_right,
    owner_slot,
    eighth,
    refresh_phase,
):
    section_no = lax.axis_index("section")
    dp_no = lax.axis_index("dp")
    mp_no = lax.axis_index("mp")
    dp_count = lax.axis_size("dp")
    mp_count = lax.axis_size("mp")
    micro_count, row_count, width = activations.shape
    tokens = micro_count * row_count
    share = tokens // mp_count
    rows, line = 2, dp_count // 4
    row_no, chip_no, core = dp_no // (2 * line), dp_no // 2 % line, dp_no % 2
    depth, shard_ff = w_up.shape[1:]
    half = shard_ff // 2
    gain_row = norm_gain[0]
    is_first = section_no == 0
    on_low_core = core == 0
    on_low_row = row_no == 0
    same_line = [
        [2 * (line * y + x) + c for x in range(line)] for y in range(rows) for c in range(2)
    ]
    swap_cores = [(i, i ^ 1) for i in range(dp_count)]
    swap_rows = [(i, (i + 2 * line) % dp_count) for i in range(dp_count)]

    first = jnp.where(is_first, w_up[0], w_down[0])
    second = jnp.where(is_first, w_down[0], w_up[0])
    both = jnp.stack([first, second])
    kept = jnp.where(on_low_core, both[:, :, :half], both[:, :, half:])
    given = jnp.where(on_low_core, both[:, :, half:], both[:, :, :half])
    taken = lax.ppermute(given, "dp", swap_cores)
    chip_rows = jnp.concatenate([kept, taken], axis=1)
    second_line = lax.all_gather(
        chip_rows[1], "dp", axis=0, axis_index_groups=same_line, tiled=True
    )
    onward, back = [
        [
            (2 * (line * y + x) + c, 2 * (line * y + (x + k) % line) + c)
            for y in range(rows) for x in range(line) for c in range(2)
        ]
        for k in (1, line - 1)
    ]
    behind = lax.ppermute(chip_rows[0], "dp", onward)
    ahead = lax.ppermute(chip_rows[0], "dp", back)
    first_line = [
        chip_rows[0], behind, lax.ppermute(behind[:depth], "dp", onward),
        lax.ppermute(ahead[depth:], "dp", back), ahead,
    ]

    act = activations.reshape(tokens, width)
    cot = cotangent.reshape(tokens, width)
    places = jnp.stack([section_no, row_no, core, chip_no]).astype(jnp.int32)

    operand = operand_step(places, act, cot, gain_row[None])
    row_operand = lax.ppermute(operand[1], "dp", swap_rows)
    core_operand = lax.ppermute(operand[0], "dp", swap_cores)
    far_operand = lax.ppermute(row_operand, "dp", swap_cores)
    mine = whole(
        functools.partial(product_kernel, line), "first_product", (4, tokens, half), places,
        operand[0], core_operand, row_operand, far_operand, *first_line,
    )
    theirs = lax.ppermute(mine, "dp", swap_rows)

    block_rows = shard_ff // BLK
    block_cols = width // BLK
    narrow = BLK // dp_count

    def by_strips(values):
        lead = values.shape[0]
        cut_up = values.reshape(lead, block_cols, dp_count, narrow)
        return cut_up.transpose(0, 2, 1, 3).reshape(lead, width)

    keep, give, halves = forward_step(
        places, mine, theirs, second_line.reshape(line, 2, depth // narrow, narrow, half)
    )
    got = lax.ppermute(give, "dp", swap_cores)
    to_mp = whole(
        join_kernel, "join", (mp_count, 2, share, width // 2), places, keep, got
    )
    second, to_mp = lax.optimization_barrier((second, to_mp))
    weight = lax.all_gather(second, "dp", axis=0, tiled=True).reshape(
        block_cols, dp_count, narrow, shard_ff
    )
    other_half = lax.ppermute(halves[1], "dp", swap_cores)
    product = jnp.concatenate(
        [
            jnp.where(on_low_core, halves[0], other_half),
            jnp.where(on_low_core, other_half, halves[0]),
        ],
        axis=1,
    )

    def sum_over_mp(partial_value):
        pieces = lax.all_to_all(
            partial_value, "mp",
            split_axis=0, concat_axis=0, tiled=True,
        )
        return jnp.sum(pieces.astype(f32), axis=0)

    def ring_over_mp(rows):
        right = [(i, (i + 1) % mp_count) for i in range(mp_count)]
        left = [((i + 1) % mp_count, i) for i in range(mp_count)]
        behind, ahead = [rows], []
        for step in range(mp_count // 2):
            behind.append(lax.ppermute(behind[-1], "mp", right))
            if step < mp_count // 2 - 1:
                ahead.append(lax.ppermute(ahead[-1] if ahead else rows, "mp", left))
        return behind + ahead[::-1]

    group_size = block_rows * block_cols
    section_owner = lax.dynamic_index_in_dim(owner_slot, section_no, 0, keepdims=False)
    local_owner = lax.dynamic_slice_in_dim(
        section_owner, mp_no * block_rows, block_rows, 0
    ).reshape(-1)
    local_slot = local_owner // mp_count
    slots = jnp.arange(group_size, dtype=jnp.int32)
    block_of_slot = jnp.sum(
        jnp.where(local_slot[None, :] == slots[:, None], slots[None, :], 0), axis=1
    )
    info = jnp.concatenate([jnp.stack([section_no, mp_no]).astype(jnp.int32), block_of_slot])

    my_rows = functools.partial(
        lax.dynamic_slice_in_dim, start_index=mp_no * share, slice_size=share, axis=0
    )
    to_mp, act, cot, gain_row = lax.optimization_barrier((to_mp, act, cot, gain_row))
    my_act = by_strips(my_rows(act))
    my_cot = by_strips(my_rows(cot))
    gain_strips = by_strips(gain_row[None])
    branch = sum_over_mp(to_mp).astype(bf16)
    straight = lax.ppermute(
        branch[0], ("section", "dp"), [(i, dp_count + i) for i in range(dp_count)]
    )
    crossed = lax.ppermute(
        branch[1], ("section", "dp"), [(i, dp_count + j) for i, j in swap_rows]
    )
    strip_cut = (share, dp_count, 1, width // (2 * dp_count))
    low = jnp.where(on_low_row, straight, crossed).reshape(strip_cut)
    high = jnp.where(on_low_row, crossed, straight).reshape(strip_cut)
    branch_rows = jnp.concatenate([low, high], axis=2).reshape(share, width)
    layer_in = (my_act.astype(f32) + branch_rows.astype(f32)).astype(bf16)
    hidden, partial_grad = second_step(
        info, ring_over_mp(layer_in), gain_strips, product, weight
    )
    hidden_all = lax.all_gather(hidden, "dp", axis=0, tiled=True)

    grad_normed = sum_over_mp(partial_grad.reshape(mp_count, share, width))
    unused, pullback = jax.vjp(
        lambda v: normalize_values(v, gain_strips), layer_in.astype(f32)
    )
    grad_in = (my_cot.astype(f32) + pullback(grad_normed)[0]).astype(bf16)

    def strips_of(values):
        return values.reshape(share, dp_count, width // dp_count).transpose(1, 0, 2)

    arrived = lax.all_to_all(
        jnp.concatenate([strips_of(grad_in), strips_of(my_cot)], axis=0), ("section", "dp"),
        split_axis=0, concat_axis=0, tiled=True,
    )
    strip = arrived[dp_count:].reshape(dp_count * share, width // dp_count)
    strip, hidden_all = lax.optimization_barrier((strip, hidden_all))
    strips_out = strip_step(
        1.0 / math.sqrt(tokens * dp_count), info,
        hidden_all.reshape(dp_count, mp_count, share, shard_ff), ring_over_mp(strip), group_size,
    )
    turned = lax.all_to_all(strips_out, "dp", split_axis=0, concat_axis=0, tiled=True)

    section_eighth = lax.dynamic_index_in_dim(eighth, section_no, 0, keepdims=False)
    local_eighth = lax.dynamic_slice_in_dim(
        section_eighth, mp_no * block_rows, block_rows, 0
    ).reshape(-1)
    my_eighth = jnp.sum(jnp.where(local_slot == dp_no, local_eighth, 0))
    due = (my_eighth == refresh_phase[0] % 8).astype(jnp.int32)
    outs = owner_step(
        due.reshape(1), turned.reshape(BLK, BLK),
        gram_left[0, 0], gram_right[0, 0], root_left[0, 0], root_right[0, 0],
    )
    return tuple(o[None, None] for o in outs)


def solution(mesh):
    spread = P("section", ("dp", "mp"), None, None)
    return jax.shard_map(
        on_device,
        mesh=mesh,
        in_specs=(
            P(None, "dp", None),
            P(None, "dp", None),
            P("section", None),
            P("section", "dp", "mp"),
            P("section", "dp", "mp"),
            spread,
            spread,
            spread,
            spread,
            P(),
            P(),
            P(),
        ),
        out_specs=(spread,) * 5,
        check_vma=False,
    )
```

```python
import functools
import math

import jax
import jax.numpy as jnp
from jax import lax
from jax.experimental import pallas as pl
from jax.experimental.pallas import tpu as pltpu
from jax.sharding import PartitionSpec as P

BLK = 512
VMEM = 24 * 1024 * 1024

norm_epsilon = 1e-05
decay_rate = 0.9
ridge_shift = 0.001
f32 = jnp.float32
bf16 = jnp.bfloat16


def normalize_values(values, gain_row):
    inverse_rms = lax.rsqrt(jnp.mean(values * values, axis=-1, keepdims=True) + norm_epsilon)
    return values * inverse_rms * gain_row


def silu_slope(pre_act):
    sigmoid_values = jax.nn.sigmoid(pre_act)
    return sigmoid_values * (1.0 + pre_act * (1.0 - sigmoid_values))


def dot(a, b, dims=((1,), (0,))):
    return lax.dot_general(a, b, (dims, ((), ())), preferred_element_type=f32)


def operand_kernel(where_ref, act_ref, cot_ref, gain_ref, o_ref, held_ref, sem):
    wide = o_ref.shape[2]
    mine = pl.ds(pl.multiple_of(where_ref[1] * wide, wide), wide)
    others = pl.ds(pl.multiple_of((1 - where_ref[1]) * wide, wide), wide)

    @pl.when(where_ref[0] == 0)
    def _():
        copy = pltpu.make_async_copy(act_ref, held_ref, sem)
        copy.start()
        copy.wait()
        normed = normalize_values(held_ref[...].astype(f32), gain_ref[...])
        held_ref[...] = normed.astype(bf16)

    @pl.when(where_ref[0] != 0)
    def _():
        copy = pltpu.make_async_copy(cot_ref, held_ref, sem)
        copy.start()
        copy.wait()

    o_ref[0] = held_ref[:, mine]
    o_ref[1] = held_ref[:, others]


def operand_step(places, act, cot, gain_row):
    tokens, width = act.shape
    vmem = pl.BlockSpec(memory_space=pltpu.VMEM)
    away = pl.BlockSpec(memory_space=pltpu.HBM)
    return pl.pallas_call(
        operand_kernel,
        in_specs=[pl.BlockSpec(memory_space=pltpu.SMEM), away, away, vmem],
        out_specs=vmem,
        out_shape=jax.ShapeDtypeStruct((2, tokens, width // 2), bf16),
        scratch_shapes=[pltpu.VMEM((tokens, width), bf16), pltpu.SemaphoreType.DMA],
        compiler_params=pltpu.CompilerParams(vmem_limit_bytes=VMEM),
        name="operand",
    )(places, act, cot, gain_row)


def product_kernel(line, where_ref, *refs):
    operands, weights, o_ref = refs[:4], refs[4:-1], refs[-1]
    core, x = where_ref[2], where_ref[3]
    depth = weights[0].shape[0] // 2
    own, behind, far_own, far_other, ahead = weights
    pieces = (
        (0, 0, own, 0), (0, 1, own, depth), (1, 0, behind, 0), (1, 1, behind, depth),
        (2, 0, far_own, 0), (2, 1, far_other, 0), (3, 0, ahead, 0), (3, 1, ahead, depth),
    )
    for g, ref in enumerate(operands):
        total = None
        for k, o, w_ref, down in pieces:
            chip, c = (x + line - k) % line, (core, 1 - core)[o]
            at = pl.multiple_of((2 * chip + c) * depth, depth)
            term = dot(ref[:, pl.ds(at, depth)], w_ref[down : down + depth, :])
            total = term if total is None else total + term
        o_ref[g] = total.astype(bf16)


def whole(kernel, name, shape, numbers, *arrays):
    vmem = pl.BlockSpec(memory_space=pltpu.VMEM)
    return pl.pallas_call(
        kernel,
        in_specs=[pl.BlockSpec(memory_space=pltpu.SMEM)] + [vmem] * len(arrays),
        out_specs=vmem,
        out_shape=jax.ShapeDtypeStruct(shape, bf16),
        compiler_params=pltpu.CompilerParams(vmem_limit_bytes=VMEM),
        name=name,
    )(numbers, *arrays)


def sigmoid(v):
    return 1.0 / (1.0 + jnp.exp(-v))


def rows_of(w_ref, e):
    part = w_ref[:, e]
    return part.reshape(part.shape[0] * part.shape[1], part.shape[2])


def forward_kernel(where_ref, mine_ref, theirs_ref, away_ref, keep_ref, give_ref, half_ref, w_ref, sems):
    core = where_ref[2]
    groups, tokens, half = mine_ref.shape
    copies = [
        pltpu.make_async_copy(away_ref.at[x], w_ref.at[x], sems.at[x]) for x in range(w_ref.shape[0])
    ]
    for copy in copies:
        copy.start()
    pieces = []
    for g in range(groups):
        total = mine_ref[g].astype(f32) + theirs_ref[(g + 2) % groups].astype(f32)
        hidden = (total * sigmoid(total)).astype(bf16)
        if g < 2:
            half_ref[g] = jnp.where(where_ref[0] == 0, hidden, total.astype(bf16))
        pieces.append(hidden)
    hidden = jnp.concatenate(pieces, axis=0)
    for copy in copies:
        copy.wait()
    line, cores, strips, narrow, _ = w_ref.shape
    wide = line * narrow
    for o, c in enumerate((core, 1 - core)):
        for e in range(0, strips, 2):
            rows = [w_ref[:, o, e + k].reshape(wide, half) for k in range(2)]
            value = dot(hidden, jnp.concatenate(rows, axis=0), ((1,), (1,))).astype(bf16)
            value = value.reshape(groups, tokens, 2 * wide)
            to = pl.ds(pl.multiple_of((c * strips + e) * wide, 2 * wide), 2 * wide)
            keep_ref[0, :, to] = value[0]
            keep_ref[1, :, to] = value[2]
            give_ref[0, :, to] = value[1]
            give_ref[1, :, to] = value[3]


def forward_step(places, mine, theirs, weight):
    groups, tokens, half = mine.shape
    line, cores, strips, narrow, _ = weight.shape
    vmem = pl.BlockSpec(memory_space=pltpu.VMEM)
    wide = jax.ShapeDtypeStruct((2, tokens, line * cores * strips * narrow), bf16)
    return pl.pallas_call(
        forward_kernel,
        in_specs=[
            pl.BlockSpec(memory_space=pltpu.SMEM), vmem, vmem, pl.BlockSpec(memory_space=pltpu.HBM)
        ],
        out_specs=[vmem] * 3,
        out_shape=[wide, wide, jax.ShapeDtypeStruct((2, tokens, half), bf16)],
        scratch_shapes=[pltpu.VMEM(weight.shape, bf16), pltpu.SemaphoreType.DMA((line,))],
        compiler_params=pltpu.CompilerParams(vmem_limit_bytes=VMEM),
        name="forward_step",
    )(places, mine, theirs, weight)


def join_kernel(where_ref, keep_ref, got_ref, o_ref):
    count, groups, share, _ = o_ref.shape
    for g in range(groups):
        total = (keep_ref[g].astype(f32) + got_ref[g].astype(f32)).astype(bf16)
        for k in range(count):
            o_ref[k, g] = total[k * share : (k + 1) * share, :]


def second_kernel(info_ref, gain_ref, product_ref, w_ref, *refs):
    chunks = refs[:-6]
    hidden_ref, out_ref, normed_ref, pre_ref, held_ref, sems = refs[-6:]
    count, share = len(chunks), chunks[0].shape[0]
    steps, block_cols, strips, narrow, _ = held_ref.shape
    wide = block_cols * narrow

    copies = [
        pltpu.make_async_copy(w_ref.at[:, pl.ds(i * strips, strips)], held_ref.at[i], sems.at[i])
        for i in range(steps)
    ]
    for copy in copies:
        copy.start()
    for k in range(count):
        place = pl.multiple_of(((info_ref[1] + count - k) % count) * share, share)
        normed = normalize_values(chunks[k][...].astype(f32), gain_ref[...])
        normed_ref[pl.ds(place, share), :] = normed.astype(bf16)
    for i in range(steps):
        copies[i].wait()
        total = None if i == 0 else pre_ref[...]
        for e in range(strips):
            at = (i * strips + e) * wide
            rows = held_ref[i, :, e].reshape(wide, held_ref.shape[4])
            term = dot(normed_ref[:, at : at + wide], rows)
            total = term if total is None else total + term
        pre_ref[...] = total
    pre = pre_ref[...]
    gate = sigmoid(pre)
    hidden_ref[...] = jnp.where(info_ref[0] == 0, product_ref[...], (pre * gate).astype(bf16))
    grad = (product_ref[...].astype(f32) * (gate * (1.0 + pre * (1.0 - gate)))).astype(bf16)
    for i in range(steps):
        for e in range(strips):
            at = (i * strips + e) * wide
            rows = held_ref[i, :, e].reshape(wide, held_ref.shape[4])
            out_ref[:, at : at + wide] = dot(grad, rows, ((1,), (1,))).astype(bf16)


def second_step(info, chunks, gain_row, product, weight):
    tokens, ff = product.shape
    block_cols, strips, narrow, _ = weight.shape
    width = strips * block_cols * narrow
    each = 2
    steps = strips // each
    vmem = pl.BlockSpec(memory_space=pltpu.VMEM)
    return pl.pallas_call(
        second_kernel,
        in_specs=[
            pl.BlockSpec(memory_space=pltpu.SMEM), vmem, vmem, pl.BlockSpec(memory_space=pltpu.HBM)
        ]
        + [vmem] * len(chunks),
        out_specs=[vmem, vmem],
        out_shape=[
            jax.ShapeDtypeStruct((tokens, ff), bf16),
            jax.ShapeDtypeStruct((tokens, width), bf16),
        ],
        scratch_shapes=[
            pltpu.VMEM((tokens, width), bf16),
            pltpu.VMEM((tokens, ff), f32),
            pltpu.VMEM((steps, block_cols, each, narrow, ff), bf16),
            pltpu.SemaphoreType.DMA((steps,)),
        ],
        compiler_params=pltpu.CompilerParams(vmem_limit_bytes=48 * 1024 * 1024),
        name="second_step",
    )(info, gain_row, product, weight, *chunks)


def strip_products(places, info_ref, hidden_ref, chunks, total_ref, held_ref, sems, fresh):
    count = hidden_ref.shape[1]
    _, replicas, share, ff = held_ref.shape
    copies = [
        pltpu.make_async_copy(
            hidden_ref.at[:, lax.rem(info_ref[1] + count - k, count)], held_ref.at[n], sems.at[n]
        )
        for n, k in enumerate(places)
    ]
    for copy in copies:
        copy.start()
    for n, chunk in enumerate(chunks):
        copies[n].wait()
        value = dot(chunk[...], held_ref[n].reshape(replicas * share, ff), ((0,), (0,)))
        if fresh and n == 0:
            total_ref[...] = value
        else:
            total_ref[...] += value


def near_kernel(places, info_ref, hidden_ref, *refs):
    strip_products(places, info_ref, hidden_ref, refs[:-3], *refs[-3:], True)


def far_kernel(places, scale, block_cols, info_ref, hidden_ref, near_ref, *refs):
    chunks, (out_ref, total_ref, held_ref, sems) = refs[:-4], refs[-4:]
    slots, narrow, _ = out_ref.shape
    total_ref[...] = near_ref[...]
    strip_products(places, info_ref, hidden_ref, chunks, total_ref, held_ref, sems, False)
    for t in range(slots):
        block = info_ref[2 + t]
        down = pl.multiple_of((block % block_cols) * narrow, narrow)
        across = pl.multiple_of((block // block_cols) * BLK, BLK)
        out_ref[t] = (total_ref[pl.ds(down, narrow), pl.ds(across, BLK)] * scale).astype(bf16)


def strip_step(scale, info, hidden_all, chunks, slots):
    replicas, count, share, ff = hidden_all.shape
    wide = chunks[0].shape[1]
    block_cols = slots // (ff // BLK)
    narrow = wide // block_cols
    reach = count // 2 - 2
    near = [k for k in range(count) if min(k, count - k) <= reach]
    far = [k for k in range(count) if k not in near]
    vmem = pl.BlockSpec(memory_space=pltpu.VMEM)
    away = pl.BlockSpec(memory_space=pltpu.HBM)
    numbers = pl.BlockSpec(memory_space=pltpu.SMEM)

    def held(some):
        return [
            pltpu.VMEM((len(some), replicas, share, ff), bf16), pltpu.SemaphoreType.DMA((len(some),))
        ]

    total = pl.pallas_call(
        functools.partial(near_kernel, near),
        in_specs=[numbers, away] + [vmem] * len(near),
        out_specs=vmem,
        out_shape=jax.ShapeDtypeStruct((wide, ff), f32),
        scratch_shapes=held(near),
        compiler_params=pltpu.CompilerParams(vmem_limit_bytes=VMEM),
        name="near_strips",
    )(info, hidden_all, *[chunks[k] for k in near])
    return pl.pallas_call(
        functools.partial(far_kernel, far, scale, block_cols),
        in_specs=[numbers, away, vmem] + [vmem] * len(far),
        out_specs=vmem,
        out_shape=jax.ShapeDtypeStruct((slots, narrow, BLK), bf16),
        scratch_shapes=[pltpu.VMEM((wide, ff), f32)] + held(far),
        compiler_params=pltpu.CompilerParams(vmem_limit_bytes=VMEM),
        name="strip_step",
    )(info, hidden_all, total, *[chunks[k] for k in far])


def inverse_root(matrix):
    order = matrix.shape[-1]
    row = lax.broadcasted_iota(jnp.int32, (order, order), 0)
    col = lax.broadcasted_iota(jnp.int32, (order, order), 1)
    diag = row == col
    shifted = matrix + jnp.where(diag, ridge_shift, 0.0)
    factor = 2.5 / jnp.sqrt(jnp.sum(shifted * shifted))
    moment = factor * shifted
    step = jnp.where(diag, 1.25, 0.0) - 0.25 * moment
    low = step.astype(bf16)
    square = dot(low, low).astype(bf16)
    fourth = dot(square, square).astype(bf16)
    moment = dot(fourth, moment.astype(bf16))
    last = jnp.where(diag, 1.25, 0.0) - 0.25 * moment
    root = jnp.sqrt(jnp.sqrt(factor))
    return root * dot(low, last.astype(bf16))


def owner_kernel(due_ref, grad_ref, gl_ref, gr_ref, rl_ref, rr_ref,
                 ngl_ref, ngr_ref, nrl_ref, nrr_ref, up_ref):
    turned = grad_ref[...]
    ngl_ref[...] = decay_rate * gl_ref[...] + dot(turned, turned, ((0,), (0,))) * (1.0 / BLK)
    ngr_ref[...] = decay_rate * gr_ref[...] + dot(turned, turned, ((1,), (1,))) * (1.0 / BLK)
    nrl_ref[...] = rl_ref[...]
    nrr_ref[...] = rr_ref[...]

    @pl.when(due_ref[0] == 1)
    def _():
        nrl_ref[...] = inverse_root(ngl_ref[...]).astype(bf16)
        nrr_ref[...] = inverse_root(ngr_ref[...]).astype(bf16)

    right = dot(turned, nrr_ref[...], ((0,), (0,))).astype(bf16)
    up_ref[...] = dot(nrl_ref[...], right).astype(bf16)


def owner_step(due, turned, gram_l, gram_r, root_l, root_r):
    vmem = pl.BlockSpec(memory_space=pltpu.VMEM)
    big = jax.ShapeDtypeStruct((BLK, BLK), f32)
    small = jax.ShapeDtypeStruct((BLK, BLK), bf16)
    return pl.pallas_call(
        owner_kernel,
        in_specs=[pl.BlockSpec(memory_space=pltpu.SMEM)] + [vmem] * 5,
        out_specs=[vmem] * 5,
        out_shape=[big, big, small, small, small],
        compiler_params=pltpu.CompilerParams(vmem_limit_bytes=VMEM),
        name="owner_step",
    )(due, turned, gram_l, gram_r, root_l, root_r)


def on_device(
    activations,
    cotangent,
    norm_gain,
    w_up,
    w_down,
    gram_left,
    gram_right,
    root_left,
    root_right,
    owner_slot,
    eighth,
    refresh_phase,
):
    section_no = lax.axis_index("section")
    dp_no = lax.axis_index("dp")
    mp_no = lax.axis_index("mp")
    dp_count = lax.axis_size("dp")
    mp_count = lax.axis_size("mp")
    micro_count, row_count, width = activations.shape
    tokens = micro_count * row_count
    share = tokens // mp_count
    rows, line = 2, dp_count // 4
    row_no, chip_no, core = dp_no // (2 * line), dp_no // 2 % line, dp_no % 2
    depth, shard_ff = w_up.shape[1:]
    half = shard_ff // 2
    gain_row = norm_gain[0]
    is_first = section_no == 0
    on_low_core = core == 0
    on_low_row = row_no == 0
    same_line = [
        [2 * (line * y + x) + c for x in range(line)] for y in range(rows) for c in range(2)
    ]
    swap_cores = [(i, i ^ 1) for i in range(dp_count)]
    swap_rows = [(i, (i + 2 * line) % dp_count) for i in range(dp_count)]

    first = jnp.where(is_first, w_up[0], w_down[0])
    second = jnp.where(is_first, w_down[0], w_up[0])
    both = jnp.stack([first, second])
    kept = jnp.where(on_low_core, both[:, :, :half], both[:, :, half:])
    given = jnp.where(on_low_core, both[:, :, half:], both[:, :, :half])
    taken = lax.ppermute(given, "dp", swap_cores)
    chip_rows = jnp.concatenate([kept, taken], axis=1)
    second_line = lax.all_gather(
        chip_rows[1], "dp", axis=0, axis_index_groups=same_line, tiled=True
    )
    onward, back = [
        [
            (2 * (line * y + x) + c, 2 * (line * y + (x + k) % line) + c)
            for y in range(rows) for x in range(line) for c in range(2)
        ]
        for k in (1, line - 1)
    ]
    behind = lax.ppermute(chip_rows[0], "dp", onward)
    ahead = lax.ppermute(chip_rows[0], "dp", back)
    first_line = [
        chip_rows[0], behind, lax.ppermute(behind[:depth], "dp", onward),
        lax.ppermute(ahead[depth:], "dp", back), ahead,
    ]

    act = activations.reshape(tokens, width)
    cot = cotangent.reshape(tokens, width)
    places = jnp.stack([section_no, row_no, core, chip_no]).astype(jnp.int32)

    operand = operand_step(places, act, cot, gain_row[None])
    row_operand = lax.ppermute(operand[1], "dp", swap_rows)
    core_operand = lax.ppermute(operand[0], "dp", swap_cores)
    far_operand = lax.ppermute(row_operand, "dp", swap_cores)
    mine = whole(
        functools.partial(product_kernel, line), "first_product", (4, tokens, half), places,
        operand[0], core_operand, row_operand, far_operand, *first_line,
    )
    theirs = lax.ppermute(mine, "dp", swap_rows)

    block_rows = shard_ff // BLK
    block_cols = width // BLK
    narrow = BLK // dp_count

    def by_strips(values):
        lead = values.shape[0]
        cut_up = values.reshape(lead, block_cols, dp_count, narrow)
        return cut_up.transpose(0, 2, 1, 3).reshape(lead, width)

    keep, give, halves = forward_step(
        places, mine, theirs, second_line.reshape(line, 2, depth // narrow, narrow, half)
    )
    got = lax.ppermute(give, "dp", swap_cores)
    to_mp = whole(
        join_kernel, "join", (mp_count, 2, share, width // 2), places, keep, got
    )
    second, to_mp = lax.optimization_barrier((second, to_mp))
    weight = lax.all_gather(second, "dp", axis=0, tiled=True).reshape(
        block_cols, dp_count, narrow, shard_ff
    )
    other_half = lax.ppermute(halves[1], "dp", swap_cores)
    product = jnp.concatenate(
        [
            jnp.where(on_low_core, halves[0], other_half),
            jnp.where(on_low_core, other_half, halves[0]),
        ],
        axis=1,
    )

    def sum_over_mp(partial_value):
        pieces = lax.all_to_all(
            partial_value, "mp",
            split_axis=0, concat_axis=0, tiled=True,
        )
        return jnp.sum(pieces.astype(f32), axis=0)

    def ring_over_mp(rows):
        right = [(i, (i + 1) % mp_count) for i in range(mp_count)]
        left = [((i + 1) % mp_count, i) for i in range(mp_count)]
        behind, ahead = [rows], []
        for step in range(mp_count // 2):
            behind.append(lax.ppermute(behind[-1], "mp", right))
            if step < mp_count // 2 - 1:
                ahead.append(lax.ppermute(ahead[-1] if ahead else rows, "mp", left))
        return behind + ahead[::-1]

    group_size = block_rows * block_cols
    section_owner = lax.dynamic_index_in_dim(owner_slot, section_no, 0, keepdims=False)
    local_owner = lax.dynamic_slice_in_dim(
        section_owner, mp_no * block_rows, block_rows, 0
    ).reshape(-1)
    local_slot = local_owner // mp_count
    slots = jnp.arange(group_size, dtype=jnp.int32)
    block_of_slot = jnp.sum(
        jnp.where(local_slot[None, :] == slots[:, None], slots[None, :], 0), axis=1
    )
    info = jnp.concatenate([jnp.stack([section_no, mp_no]).astype(jnp.int32), block_of_slot])

    my_rows = functools.partial(
        lax.dynamic_slice_in_dim, start_index=mp_no * share, slice_size=share, axis=0
    )
    to_mp, act, cot, gain_row = lax.optimization_barrier((to_mp, act, cot, gain_row))
    my_act = by_strips(my_rows(act))
    my_cot = by_strips(my_rows(cot))
    gain_strips = by_strips(gain_row[None])
    branch = sum_over_mp(to_mp).astype(bf16)
    straight = lax.ppermute(
        branch[0], ("section", "dp"), [(i, dp_count + i) for i in range(dp_count)]
    )
    crossed = lax.ppermute(
        branch[1], ("section", "dp"), [(i, dp_count + j) for i, j in swap_rows]
    )
    strip_cut = (share, dp_count, 1, width // (2 * dp_count))
    low = jnp.where(on_low_row, straight, crossed).reshape(strip_cut)
    high = jnp.where(on_low_row, crossed, straight).reshape(strip_cut)
    branch_rows = jnp.concatenate([low, high], axis=2).reshape(share, width)
    layer_in = (my_act.astype(f32) + branch_rows.astype(f32)).astype(bf16)
    hidden, partial_grad = second_step(
        info, ring_over_mp(layer_in), gain_strips, product, weight
    )
    hidden_all = lax.all_gather(hidden, "dp", axis=0, tiled=True)

    grad_normed = sum_over_mp(partial_grad.reshape(mp_count, share, width))
    unused, pullback = jax.vjp(
        lambda v: normalize_values(v, gain_strips), layer_in.astype(f32)
    )
    grad_in = (my_cot.astype(f32) + pullback(grad_normed)[0]).astype(bf16)

    def strips_of(values):
        return values.reshape(share, dp_count, width // dp_count).transpose(1, 0, 2)

    arrived = lax.all_to_all(
        jnp.concatenate([strips_of(grad_in), strips_of(my_cot)], axis=0), ("section", "dp"),
        split_axis=0, concat_axis=0, tiled=True,
    )
    strip = arrived[dp_count:].reshape(dp_count * share, width // dp_count)
    strip, hidden_all = lax.optimization_barrier((strip, hidden_all))
    strips_out = strip_step(
        1.0 / math.sqrt(tokens * dp_count), info,
        hidden_all.reshape(dp_count, mp_count, share, shard_ff), ring_over_mp(strip), group_size,
    )
    turned = lax.all_to_all(strips_out, "dp", split_axis=0, concat_axis=0, tiled=True)

    section_eighth = lax.dynamic_index_in_dim(eighth, section_no, 0, keepdims=False)
    local_eighth = lax.dynamic_slice_in_dim(
        section_eighth, mp_no * block_rows, block_rows, 0
    ).reshape(-1)
    my_eighth = jnp.sum(jnp.where(local_slot == dp_no, local_eighth, 0))
    due = (my_eighth == refresh_phase[0] % 8).astype(jnp.int32)
    outs = owner_step(
        due.reshape(1), turned.reshape(BLK, BLK),
        gram_left[0, 0], gram_right[0, 0], root_left[0, 0], root_right[0, 0],
    )
    return tuple(o[None, None] for o in outs)


def solution(mesh):
    spread = P("section", ("dp", "mp"), None, None)
    return jax.shard_map(
        on_device,
        mesh=mesh,
        in_specs=(
            P(None, "dp", None),
            P(None, "dp", None),
            P("section", None),
            P("section", "dp", "mp"),
            P("section", "dp", "mp"),
            spread,
            spread,
            spread,
            spread,
            P(),
            P(),
            P(),
        ),
        out_specs=(spread,) * 5,
        check_vma=False,
    )
```

```python
import functools
import math

import jax
import jax.numpy as jnp
from jax import lax
from jax.experimental import pallas as pl
from jax.experimental.pallas import tpu as pltpu
from jax.sharding import PartitionSpec as P

BLK = 512
VMEM = 24 * 1024 * 1024

norm_epsilon = 1e-05
decay_rate = 0.9
ridge_shift = 0.001
f32 = jnp.float32
bf16 = jnp.bfloat16


def normalize_values(values, gain_row):
    inverse_rms = lax.rsqrt(jnp.mean(values * values, axis=-1, keepdims=True) + norm_epsilon)
    return values * inverse_rms * gain_row


def silu_slope(pre_act):
    sigmoid_values = jax.nn.sigmoid(pre_act)
    return sigmoid_values * (1.0 + pre_act * (1.0 - sigmoid_values))


def dot(a, b, dims=((1,), (0,))):
    return lax.dot_general(a, b, (dims, ((), ())), preferred_element_type=f32)


def operand_kernel(where_ref, act_ref, cot_ref, gain_ref, o_ref, held_ref, sem):
    wide = o_ref.shape[2]
    mine = pl.ds(pl.multiple_of(where_ref[1] * wide, wide), wide)
    others = pl.ds(pl.multiple_of((1 - where_ref[1]) * wide, wide), wide)

    @pl.when(where_ref[0] == 0)
    def _():
        copy = pltpu.make_async_copy(act_ref, held_ref, sem)
        copy.start()
        copy.wait()
        normed = normalize_values(held_ref[...].astype(f32), gain_ref[...])
        held_ref[...] = normed.astype(bf16)

    @pl.when(where_ref[0] != 0)
    def _():
        copy = pltpu.make_async_copy(cot_ref, held_ref, sem)
        copy.start()
        copy.wait()

    o_ref[0] = held_ref[:, mine]
    o_ref[1] = held_ref[:, others]


def operand_step(places, act, cot, gain_row):
    tokens, width = act.shape
    vmem = pl.BlockSpec(memory_space=pltpu.VMEM)
    away = pl.BlockSpec(memory_space=pltpu.HBM)
    return pl.pallas_call(
        operand_kernel,
        in_specs=[pl.BlockSpec(memory_space=pltpu.SMEM), away, away, vmem],
        out_specs=vmem,
        out_shape=jax.ShapeDtypeStruct((2, tokens, width // 2), bf16),
        scratch_shapes=[pltpu.VMEM((tokens, width), bf16), pltpu.SemaphoreType.DMA],
        compiler_params=pltpu.CompilerParams(vmem_limit_bytes=VMEM),
        name="operand",
    )(places, act, cot, gain_row)


def product_kernel(line, where_ref, *refs):
    operands, weights, o_ref = refs[:4], refs[4:-1], refs[-1]
    core, x = where_ref[2], where_ref[3]
    depth = weights[0].shape[0] // 2
    own, behind, far_own, far_other, ahead = weights
    pieces = (
        (0, 0, own, 0), (0, 1, own, depth), (1, 0, behind, 0), (1, 1, behind, depth),
        (2, 0, far_own, 0), (2, 1, far_other, 0), (3, 0, ahead, 0), (3, 1, ahead, depth),
    )
    for g, ref in enumerate(operands):
        total = None
        for k, o, w_ref, down in pieces:
            chip, c = (x + line - k) % line, (core, 1 - core)[o]
            at = pl.multiple_of((2 * chip + c) * depth, depth)
            term = dot(ref[:, pl.ds(at, depth)], w_ref[down : down + depth, :])
            total = term if total is None else total + term
        o_ref[g] = total.astype(bf16)


def whole(kernel, name, shape, numbers, *arrays):
    vmem = pl.BlockSpec(memory_space=pltpu.VMEM)
    return pl.pallas_call(
        kernel,
        in_specs=[pl.BlockSpec(memory_space=pltpu.SMEM)] + [vmem] * len(arrays),
        out_specs=vmem,
        out_shape=jax.ShapeDtypeStruct(shape, bf16),
        compiler_params=pltpu.CompilerParams(vmem_limit_bytes=VMEM),
        name=name,
    )(numbers, *arrays)


def sigmoid(v):
    return 1.0 / (1.0 + jnp.exp(-v))


def rows_of(w_ref, e):
    part = w_ref[:, e]
    return part.reshape(part.shape[0] * part.shape[1], part.shape[2])


def forward_kernel(first, where_ref, mine_ref, theirs_ref, w_ref, out_ref, half_ref):
    core = where_ref[2]
    groups, tokens, half = mine_ref.shape
    pieces = []
    for g in (first, first + 2):
        total = mine_ref[g].astype(f32) + theirs_ref[(g + 2) % groups].astype(f32)
        hidden = (total * sigmoid(total)).astype(bf16)
        if g < 2:
            half_ref[...] = jnp.where(where_ref[0] == 0, hidden, total.astype(bf16))
        pieces.append(hidden)
    hidden = jnp.concatenate(pieces, axis=0)
    line, cores, strips, narrow, _ = w_ref.shape
    wide = line * narrow
    for o, c in enumerate((core, 1 - core)):
        for e in range(0, strips, 2):
            rows = [w_ref[:, o, e + k].reshape(wide, half) for k in range(2)]
            value = dot(hidden, jnp.concatenate(rows, axis=0), ((1,), (1,))).astype(bf16)
            to = pl.ds(pl.multiple_of((c * strips + e) * wide, 2 * wide), 2 * wide)
            out_ref[:, :, to] = value.reshape(2, tokens, 2 * wide)


def forward_step(first, places, mine, theirs, weight):
    groups, tokens, half = mine.shape
    line, cores, strips, narrow, _ = weight.shape
    vmem = pl.BlockSpec(memory_space=pltpu.VMEM)
    return pl.pallas_call(
        functools.partial(forward_kernel, first),
        in_specs=[pl.BlockSpec(memory_space=pltpu.SMEM)] + [vmem] * 3,
        out_specs=[vmem] * 2,
        out_shape=[
            jax.ShapeDtypeStruct((2, tokens, line * cores * strips * narrow), bf16),
            jax.ShapeDtypeStruct((tokens, half), bf16),
        ],
        compiler_params=pltpu.CompilerParams(vmem_limit_bytes=VMEM),
        name=("keep_step", "give_step")[first],
    )(places, mine, theirs, weight)


def join_kernel(where_ref, keep_ref, got_ref, o_ref):
    count, groups, share, _ = o_ref.shape
    for g in range(groups):
        total = (keep_ref[g].astype(f32) + got_ref[g].astype(f32)).astype(bf16)
        for k in range(count):
            o_ref[k, g] = total[k * share : (k + 1) * share, :]


def second_kernel(info_ref, gain_ref, product_ref, w_ref, *refs):
    chunks = refs[:-6]
    hidden_ref, out_ref, normed_ref, pre_ref, held_ref, sems = refs[-6:]
    count, share = len(chunks), chunks[0].shape[0]
    steps, block_cols, strips, narrow, _ = held_ref.shape
    wide = block_cols * narrow

    copies = [
        pltpu.make_async_copy(w_ref.at[:, pl.ds(i * strips, strips)], held_ref.at[i], sems.at[i])
        for i in range(steps)
    ]
    for copy in copies:
        copy.start()
    for k in range(count):
        place = pl.multiple_of(((info_ref[1] + count - k) % count) * share, share)
        normed = normalize_values(chunks[k][...].astype(f32), gain_ref[...])
        normed_ref[pl.ds(place, share), :] = normed.astype(bf16)
    for i in range(steps):
        copies[i].wait()
        total = None if i == 0 else pre_ref[...]
        for e in range(strips):
            at = (i * strips + e) * wide
            rows = held_ref[i, :, e].reshape(wide, held_ref.shape[4])
            term = dot(normed_ref[:, at : at + wide], rows)
            total = term if total is None else total + term
        pre_ref[...] = total
    pre = pre_ref[...]
    gate = sigmoid(pre)
    hidden_ref[...] = jnp.where(info_ref[0] == 0, product_ref[...], (pre * gate).astype(bf16))
    grad = (product_ref[...].astype(f32) * (gate * (1.0 + pre * (1.0 - gate)))).astype(bf16)
    for i in range(steps):
        for e in range(strips):
            at = (i * strips + e) * wide
            rows = held_ref[i, :, e].reshape(wide, held_ref.shape[4])
            out_ref[:, at : at + wide] = dot(grad, rows, ((1,), (1,))).astype(bf16)


def second_step(info, chunks, gain_row, product, weight):
    tokens, ff = product.shape
    block_cols, strips, narrow, _ = weight.shape
    width = strips * block_cols * narrow
    each = 2
    steps = strips // each
    vmem = pl.BlockSpec(memory_space=pltpu.VMEM)
    return pl.pallas_call(
        second_kernel,
        in_specs=[
            pl.BlockSpec(memory_space=pltpu.SMEM), vmem, vmem, pl.BlockSpec(memory_space=pltpu.HBM)
        ]
        + [vmem] * len(chunks),
        out_specs=[vmem, vmem],
        out_shape=[
            jax.ShapeDtypeStruct((tokens, ff), bf16),
            jax.ShapeDtypeStruct((tokens, width), bf16),
        ],
        scratch_shapes=[
            pltpu.VMEM((tokens, width), bf16),
            pltpu.VMEM((tokens, ff), f32),
            pltpu.VMEM((steps, block_cols, each, narrow, ff), bf16),
            pltpu.SemaphoreType.DMA((steps,)),
        ],
        compiler_params=pltpu.CompilerParams(vmem_limit_bytes=48 * 1024 * 1024),
        name="second_step",
    )(info, gain_row, product, weight, *chunks)


def strip_products(places, info_ref, hidden_ref, chunks, total_ref, held_ref, sems, fresh):
    count = hidden_ref.shape[1]
    _, replicas, share, ff = held_ref.shape
    copies = [
        pltpu.make_async_copy(
            hidden_ref.at[:, lax.rem(info_ref[1] + count - k, count)], held_ref.at[n], sems.at[n]
        )
        for n, k in enumerate(places)
    ]
    for copy in copies:
        copy.start()
    for n, chunk in enumerate(chunks):
        copies[n].wait()
        value = dot(chunk[...], held_ref[n].reshape(replicas * share, ff), ((0,), (0,)))
        if fresh and n == 0:
            total_ref[...] = value
        else:
            total_ref[...] += value


def near_kernel(places, info_ref, hidden_ref, *refs):
    strip_products(places, info_ref, hidden_ref, refs[:-3], *refs[-3:], True)


def far_kernel(places, scale, block_cols, info_ref, hidden_ref, near_ref, *refs):
    chunks, (out_ref, total_ref, held_ref, sems) = refs[:-4], refs[-4:]
    slots, narrow, _ = out_ref.shape
    total_ref[...] = near_ref[...]
    strip_products(places, info_ref, hidden_ref, chunks, total_ref, held_ref, sems, False)
    for t in range(slots):
        block = info_ref[2 + t]
        down = pl.multiple_of((block % block_cols) * narrow, narrow)
        across = pl.multiple_of((block // block_cols) * BLK, BLK)
        out_ref[t] = (total_ref[pl.ds(down, narrow), pl.ds(across, BLK)] * scale).astype(bf16)


def strip_step(scale, info, hidden_all, chunks, slots):
    replicas, count, share, ff = hidden_all.shape
    wide = chunks[0].shape[1]
    block_cols = slots // (ff // BLK)
    narrow = wide // block_cols
    reach = count // 2 - 2
    near = [k for k in range(count) if min(k, count - k) <= reach]
    far = [k for k in range(count) if k not in near]
    vmem = pl.BlockSpec(memory_space=pltpu.VMEM)
    away = pl.BlockSpec(memory_space=pltpu.HBM)
    numbers = pl.BlockSpec(memory_space=pltpu.SMEM)

    def held(some):
        return [
            pltpu.VMEM((len(some), replicas, share, ff), bf16), pltpu.SemaphoreType.DMA((len(some),))
        ]

    total = pl.pallas_call(
        functools.partial(near_kernel, near),
        in_specs=[numbers, away] + [vmem] * len(near),
        out_specs=vmem,
        out_shape=jax.ShapeDtypeStruct((wide, ff), f32),
        scratch_shapes=held(near),
        compiler_params=pltpu.CompilerParams(vmem_limit_bytes=VMEM),
        name="near_strips",
    )(info, hidden_all, *[chunks[k] for k in near])
    return pl.pallas_call(
        functools.partial(far_kernel, far, scale, block_cols),
        in_specs=[numbers, away, vmem] + [vmem] * len(far),
        out_specs=vmem,
        out_shape=jax.ShapeDtypeStruct((slots, narrow, BLK), bf16),
        scratch_shapes=[pltpu.VMEM((wide, ff), f32)] + held(far),
        compiler_params=pltpu.CompilerParams(vmem_limit_bytes=VMEM),
        name="strip_step",
    )(info, hidden_all, total, *[chunks[k] for k in far])


def inverse_root(matrix):
    order = matrix.shape[-1]
    row = lax.broadcasted_iota(jnp.int32, (order, order), 0)
    col = lax.broadcasted_iota(jnp.int32, (order, order), 1)
    diag = row == col
    shifted = matrix + jnp.where(diag, ridge_shift, 0.0)
    factor = 2.5 / jnp.sqrt(jnp.sum(shifted * shifted))
    moment = factor * shifted
    step = jnp.where(diag, 1.25, 0.0) - 0.25 * moment
    low = step.astype(bf16)
    square = dot(low, low).astype(bf16)
    fourth = dot(square, square).astype(bf16)
    moment = dot(fourth, moment.astype(bf16))
    last = jnp.where(diag, 1.25, 0.0) - 0.25 * moment
    root = jnp.sqrt(jnp.sqrt(factor))
    return root * dot(low, last.astype(bf16))


def owner_kernel(due_ref, grad_ref, gl_ref, gr_ref, rl_ref, rr_ref,
                 ngl_ref, ngr_ref, nrl_ref, nrr_ref, up_ref):
    turned = grad_ref[...]
    ngl_ref[...] = decay_rate * gl_ref[...] + dot(turned, turned, ((0,), (0,))) * (1.0 / BLK)
    ngr_ref[...] = decay_rate * gr_ref[...] + dot(turned, turned, ((1,), (1,))) * (1.0 / BLK)
    nrl_ref[...] = rl_ref[...]
    nrr_ref[...] = rr_ref[...]

    @pl.when(due_ref[0] == 1)
    def _():
        nrl_ref[...] = inverse_root(ngl_ref[...]).astype(bf16)
        nrr_ref[...] = inverse_root(ngr_ref[...]).astype(bf16)

    right = dot(turned, nrr_ref[...], ((0,), (0,))).astype(bf16)
    up_ref[...] = dot(nrl_ref[...], right).astype(bf16)


def owner_step(due, turned, gram_l, gram_r, root_l, root_r):
    vmem = pl.BlockSpec(memory_space=pltpu.VMEM)
    big = jax.ShapeDtypeStruct((BLK, BLK), f32)
    small = jax.ShapeDtypeStruct((BLK, BLK), bf16)
    return pl.pallas_call(
        owner_kernel,
        in_specs=[pl.BlockSpec(memory_space=pltpu.SMEM)] + [vmem] * 5,
        out_specs=[vmem] * 5,
        out_shape=[big, big, small, small, small],
        compiler_params=pltpu.CompilerParams(vmem_limit_bytes=VMEM),
        name="owner_step",
    )(due, turned, gram_l, gram_r, root_l, root_r)


def on_device(
    activations,
    cotangent,
    norm_gain,
    w_up,
    w_down,
    gram_left,
    gram_right,
    root_left,
    root_right,
    owner_slot,
    eighth,
    refresh_phase,
):
    section_no = lax.axis_index("section")
    dp_no = lax.axis_index("dp")
    mp_no = lax.axis_index("mp")
    dp_count = lax.axis_size("dp")
    mp_count = lax.axis_size("mp")
    micro_count, row_count, width = activations.shape
    tokens = micro_count * row_count
    share = tokens // mp_count
    rows, line = 2, dp_count // 4
    row_no, chip_no, core = dp_no // (2 * line), dp_no // 2 % line, dp_no % 2
    depth, shard_ff = w_up.shape[1:]
    half = shard_ff // 2
    gain_row = norm_gain[0]
    is_first = section_no == 0
    on_low_core = core == 0
    on_low_row = row_no == 0
    same_line = [
        [2 * (line * y + x) + c for x in range(line)] for y in range(rows) for c in range(2)
    ]
    swap_cores = [(i, i ^ 1) for i in range(dp_count)]
    swap_rows = [(i, (i + 2 * line) % dp_count) for i in range(dp_count)]

    first = jnp.where(is_first, w_up[0], w_down[0])
    second = jnp.where(is_first, w_down[0], w_up[0])
    both = jnp.stack([first, second])
    kept = jnp.where(on_low_core, both[:, :, :half], both[:, :, half:])
    given = jnp.where(on_low_core, both[:, :, half:], both[:, :, :half])
    taken = lax.ppermute(given, "dp", swap_cores)
    chip_rows = jnp.concatenate([kept, taken], axis=1)
    second_line = lax.all_gather(
        chip_rows[1], "dp", axis=0, axis_index_groups=same_line, tiled=True
    )
    onward, back = [
        [
            (2 * (line * y + x) + c, 2 * (line * y + (x + k) % line) + c)
            for y in range(rows) for x in range(line) for c in range(2)
        ]
        for k in (1, line - 1)
    ]
    behind = lax.ppermute(chip_rows[0], "dp", onward)
    ahead = lax.ppermute(chip_rows[0], "dp", back)
    first_line = [
        chip_rows[0], behind, lax.ppermute(behind[:depth], "dp", onward),
        lax.ppermute(ahead[depth:], "dp", back), ahead,
    ]

    act = activations.reshape(tokens, width)
    cot = cotangent.reshape(tokens, width)
    places = jnp.stack([section_no, row_no, core, chip_no]).astype(jnp.int32)

    operand = operand_step(places, act, cot, gain_row[None])
    row_operand = lax.ppermute(operand[1], "dp", swap_rows)
    core_operand = lax.ppermute(operand[0], "dp", swap_cores)
    far_operand = lax.ppermute(row_operand, "dp", swap_cores)
    mine = whole(
        functools.partial(product_kernel, line), "first_product", (4, tokens, half), places,
        operand[0], core_operand, row_operand, far_operand, *first_line,
    )
    theirs = lax.ppermute(mine, "dp", swap_rows)

    block_rows = shard_ff // BLK
    block_cols = width // BLK
    narrow = BLK // dp_count

    def by_strips(values):
        lead = values.shape[0]
        cut_up = values.reshape(lead, block_cols, dp_count, narrow)
        return cut_up.transpose(0, 2, 1, 3).reshape(lead, width)

    line_weight = second_line.reshape(line, 2, depth // narrow, narrow, half)
    give, given_half = forward_step(1, places, mine, theirs, line_weight)
    keep, kept_half = forward_step(0, places, mine, theirs, line_weight)
    got = lax.ppermute(give, "dp", swap_cores)
    to_mp = whole(
        join_kernel, "join", (mp_count, 2, share, width // 2), places, keep, got
    )
    second, to_mp = lax.optimization_barrier((second, to_mp))
    weight = lax.all_gather(second, "dp", axis=0, tiled=True).reshape(
        block_cols, dp_count, narrow, shard_ff
    )
    other_half = lax.ppermute(given_half, "dp", swap_cores)
    product = jnp.concatenate(
        [
            jnp.where(on_low_core, kept_half, other_half),
            jnp.where(on_low_core, other_half, kept_half),
        ],
        axis=1,
    )

    def sum_over_mp(partial_value):
        pieces = lax.all_to_all(
            partial_value, "mp",
            split_axis=0, concat_axis=0, tiled=True,
        )
        return jnp.sum(pieces.astype(f32), axis=0)

    def ring_over_mp(rows):
        right = [(i, (i + 1) % mp_count) for i in range(mp_count)]
        left = [((i + 1) % mp_count, i) for i in range(mp_count)]
        behind, ahead = [rows], []
        for step in range(mp_count // 2):
            behind.append(lax.ppermute(behind[-1], "mp", right))
            if step < mp_count // 2 - 1:
                ahead.append(lax.ppermute(ahead[-1] if ahead else rows, "mp", left))
        return behind + ahead[::-1]

    group_size = block_rows * block_cols
    section_owner = lax.dynamic_index_in_dim(owner_slot, section_no, 0, keepdims=False)
    local_owner = lax.dynamic_slice_in_dim(
        section_owner, mp_no * block_rows, block_rows, 0
    ).reshape(-1)
    local_slot = local_owner // mp_count
    slots = jnp.arange(group_size, dtype=jnp.int32)
    block_of_slot = jnp.sum(
        jnp.where(local_slot[None, :] == slots[:, None], slots[None, :], 0), axis=1
    )
    info = jnp.concatenate([jnp.stack([section_no, mp_no]).astype(jnp.int32), block_of_slot])

    my_rows = functools.partial(
        lax.dynamic_slice_in_dim, start_index=mp_no * share, slice_size=share, axis=0
    )
    to_mp, act, cot, gain_row = lax.optimization_barrier((to_mp, act, cot, gain_row))
    my_act = by_strips(my_rows(act))
    my_cot = by_strips(my_rows(cot))
    gain_strips = by_strips(gain_row[None])
    branch = sum_over_mp(to_mp).astype(bf16)
    straight = lax.ppermute(
        branch[0], ("section", "dp"), [(i, dp_count + i) for i in range(dp_count)]
    )
    crossed = lax.ppermute(
        branch[1], ("section", "dp"), [(i, dp_count + j) for i, j in swap_rows]
    )
    strip_cut = (share, dp_count, 1, width // (2 * dp_count))
    low = jnp.where(on_low_row, straight, crossed).reshape(strip_cut)
    high = jnp.where(on_low_row, crossed, straight).reshape(strip_cut)
    branch_rows = jnp.concatenate([low, high], axis=2).reshape(share, width)
    layer_in = (my_act.astype(f32) + branch_rows.astype(f32)).astype(bf16)
    hidden, partial_grad = second_step(
        info, ring_over_mp(layer_in), gain_strips, product, weight
    )
    hidden_all = lax.all_gather(hidden, "dp", axis=0, tiled=True)

    grad_normed = sum_over_mp(partial_grad.reshape(mp_count, share, width))
    unused, pullback = jax.vjp(
        lambda v: normalize_values(v, gain_strips), layer_in.astype(f32)
    )
    grad_in = (my_cot.astype(f32) + pullback(grad_normed)[0]).astype(bf16)

    def strips_of(values):
        return values.reshape(share, dp_count, width // dp_count).transpose(1, 0, 2)

    arrived = lax.all_to_all(
        jnp.concatenate([strips_of(grad_in), strips_of(my_cot)], axis=0), ("section", "dp"),
        split_axis=0, concat_axis=0, tiled=True,
    )
    strip = arrived[dp_count:].reshape(dp_count * share, width // dp_count)
    strip, hidden_all = lax.optimization_barrier((strip, hidden_all))
    strips_out = strip_step(
        1.0 / math.sqrt(tokens * dp_count), info,
        hidden_all.reshape(dp_count, mp_count, share, shard_ff), ring_over_mp(strip), group_size,
    )
    turned = lax.all_to_all(strips_out, "dp", split_axis=0, concat_axis=0, tiled=True)

    section_eighth = lax.dynamic_index_in_dim(eighth, section_no, 0, keepdims=False)
    local_eighth = lax.dynamic_slice_in_dim(
        section_eighth, mp_no * block_rows, block_rows, 0
    ).reshape(-1)
    my_eighth = jnp.sum(jnp.where(local_slot == dp_no, local_eighth, 0))
    due = (my_eighth == refresh_phase[0] % 8).astype(jnp.int32)
    outs = owner_step(
        due.reshape(1), turned.reshape(BLK, BLK),
        gram_left[0, 0], gram_right[0, 0], root_left[0, 0], root_right[0, 0],
    )
    return tuple(o[None, None] for o in outs)


def solution(mesh):
    spread = P("section", ("dp", "mp"), None, None)
    return jax.shard_map(
        on_device,
        mesh=mesh,
        in_specs=(
            P(None, "dp", None),
            P(None, "dp", None),
            P("section", None),
            P("section", "dp", "mp"),
            P("section", "dp", "mp"),
            spread,
            spread,
            spread,
            spread,
            P(),
            P(),
            P(),
        ),
        out_specs=(spread,) * 5,
        check_vma=False,
    )
```
